256 devices in a mesh: ctx: 16 (over z, core), ep: 16 (over x, y).
Axes of the slice: x: 4, y: 4, z: 8, core: 2. Of those that a mesh axis runs over, the one named last changes fastest.
Arguments:
- residual: bfloat16 [16384, 2048], P(('ctx', 'ep')), may hold values from -6 to 6
- query_states: bfloat16 [16384, 2048], P('ctx', 'ep'), may hold values from -5 to 5
- key_states: bfloat16 [16384, 512], P('ctx'), may hold values from -5 to 5
- value_states: bfloat16 [16384, 512], P('ctx'), may hold values from -6 to 6
- out_proj: bfloat16 [2048, 2048], P('ep'), may hold values from -0.125 to 0.125
- norm_gain: float32 [2048], replicated, may hold values from 0.25 to 1.75
- w_gate: bfloat16 [256, 2048, 384], P(('ctx', 'ep')), may hold values from -0.125 to 0.125
- w_up: bfloat16 [256, 2048, 384], P(('ctx', 'ep')), may hold values from -0.125 to 0.125
- w_down: bfloat16 [256, 384, 2048], P(('ctx', 'ep')), may hold values from -0.21875 to 0.21875
- expert_ids: int32 [16384, 8], P(('ctx', 'ep')), may hold values from 0 to 127, all different within a row; in each aligned block of 64 rows (0 to 63, 64 to 127, ...) at most 6 rows name the same one
- route_weights: float32 [16384, 8], P(('ctx', 'ep')), may hold values from 0.05 to 1
Outputs:
- layer_out: bfloat16 [16384, 2048], P(('ctx', 'ep'))
The draws below stay inside these ranges and needn't reach their ends.
Inputs may be any that keep to these rules, and one draw needn't show every extreme that they name: `expert_ids`: among the rows of one device no expert is named more than 6 times.
All inputs are finite; a program needn't handle non-finite values.
Results may differ from the reference program's by a relative error of at most 0.018.
Values may be sent and summed in bfloat16 or wider, within the bound.
No kernel may reach another device: no remote copies, remote signals or barrier semaphores. Data moves between devices by JAX's collectives and lax.ppermute only.
A program may use at most 64 MiB of HBM per device.

```python
import math
import jax
import jax.numpy as jnp
import numpy as np
from jax import lax

D = 2048
HD = 128
KVH = 4
HQ = 16
EXPERTS = 128
TOP = 8
FF_E = 768
TOK_DEV = 64
HALF = 384
CAP = 6
TOK_CTX = 1024
TOKENS = 16384
N_CTX = 16
N_EP = 16


def draw_query_states(key, part):
    key = jax.random.fold_in(key, 1)
    base = jnp.clip(jax.random.normal(key, (TOKENS, HQ * HD), jnp.float32), -5.0, 5.0)
    return base.astype(jnp.bfloat16)


def draw_key_states(key, part):
    key = jax.random.fold_in(key, 2)
    base = jnp.clip(jax.random.normal(key, (TOKENS, KVH * HD), jnp.float32), -5.0, 5.0)
    return base.astype(jnp.bfloat16)


def block_scale(rng, extent, shards, least, high):
    def one(axis_at, parts):
        heights = jax.random.uniform(jax.random.fold_in(jax.random.fold_in(rng, 6), axis_at), (parts,), jnp.float32, least / len(shards), high / len(shards))
        return jnp.repeat(jnp.exp(heights), extent[axis_at] // parts).reshape((-1,) + (1,) * (len(extent) - axis_at - 1))

    level = one(*shards[0])
    for cut in shards[1:]:
        level = level * one(*cut)
    return level


def deal_out(stream_key, own, number, rows, count, top, limit, slope):
    order = jax.random.permutation(stream_key, count)
    heavy_load, usual = load_shares(count, rows * top, limit, slope, True), load_shares(count, rows * top, limit, slope, False)
    places = jnp.arange(count)

    def named(lengths, rotation):
        used = int((lengths > 0).sum())
        fixed = max(1, used // 4)
        passed = fixed + (places - fixed + rotation * (used - fixed)) % max(1, count - fixed)
        return jnp.zeros((count,), jnp.int32).at[order[jnp.where(places < fixed, places, passed)]].set(jnp.asarray(lengths, jnp.int32))

    lengths = jnp.where(number % 4 == 0, named(heavy_load, number // 4), named(usual, number - number // 4 - 1))
    mixed = jax.random.permutation(jax.random.fold_in(own, 3), count)
    donor, receiver = mixed[0:count // 2 * 2:2], mixed[1:count // 2 * 2:2]
    slack = jnp.minimum(lengths[donor] - 1, limit - lengths[receiver]) // 2
    slack = jnp.where((donor == order[0]) | (receiver == order[0]) | (lengths[receiver] == 0), 0, jnp.maximum(slack, 0))
    passed = jax.random.randint(jax.random.fold_in(own, 4), (count // 2,), 0, 1 << 20) % (slack + 1)
    lengths = lengths.at[donor].add(-passed).at[receiver].add(passed)
    members = jnp.searchsorted(jnp.cumsum(lengths), jnp.arange(rows * top), side="right").astype(jnp.int32)
    table = members.reshape(top, rows).T
    table = table[jax.random.permutation(jax.random.fold_in(own, 1), rows)]
    rotation = jax.random.randint(jax.random.fold_in(own, 2), (rows, 1), 0, top)
    return jnp.take_along_axis(table, (jnp.arange(top)[None, :] + rotation) % top, axis=1)


def load_shares(amount, total, most, lean, full):
    weights = [(1 << 20) // math.isqrt(grade ** lean) + 1 for grade in range(1, amount + 1)]
    largest = most if full else min(most, max(-(-total // amount), total * weights[0] // sum(weights)))
    least = 1 if total - largest >= amount - 1 else 0
    given, spare = [largest] + [least] * (amount - 1), total - largest - least * (amount - 1)
    while spare > 0:
        candidates = [i for i in range(1, amount) if given[i] < largest] or [i for i in range(1, amount) if given[i] < most]
        pool, remaining = sum([weights[i] for i in candidates]), spare
        for i in candidates:
            more = min(most - given[i], max(1, remaining * weights[i] // pool), spare)
            given[i] = given[i] + more
            spare = spare - more
    return np.array(given)


def normal_values(key, extent, spread, most, split=(), kind=jnp.bfloat16):
    drawn = spread * jax.random.normal(key, extent, jnp.float32)
    if split:
        drawn = drawn * block_scale(key, extent, split, -0.22, 0.18)
    return jnp.clip(drawn, -most, most).astype(kind)


def setup_inputs(seed: int = 0) -> dict:
    streams_of = jax.random.split(jax.random.key(seed), 12)
    residual = normal_values(streams_of[0], (TOKENS, D), 1.0, 6.0, ((0, 256),))
    query_states = draw_query_states(jax.random.fold_in(streams_of[11], 71), 0)
    key_states = draw_key_states(jax.random.fold_in(streams_of[11], 71), 0)
    value_states = normal_values(streams_of[3], (TOKENS, KVH * HD), 1.0, 6.0, ((0, 16),))
    out_proj = normal_values(streams_of[4], (HQ * HD, D), (HQ * HD) ** -0.5, 0.125, ((0, 16),))
    norm_gain = jnp.clip(1.0 + 0.15 * jax.random.normal(streams_of[5], (D,), jnp.float32), 0.25, 1.75)
    w_gate = normal_values(streams_of[6], (2 * EXPERTS, D, HALF), D ** -0.5, 0.125, ((0, 256),))
    w_up = normal_values(streams_of[7], (2 * EXPERTS, D, HALF), D ** -0.5, 0.125, ((0, 256),))
    w_down = normal_values(streams_of[8], (2 * EXPERTS, HALF, D), FF_E ** -0.5, 0.21875, ((0, 256),))
    expert_ids_keys = jax.random.split(jax.random.fold_in(streams_of[9], 1), TOKENS // TOK_DEV)
    expert_ids_turns = jax.random.permutation(jax.random.fold_in(streams_of[9], 3), TOKENS // TOK_DEV)
    expert_ids = jax.vmap(lambda own, number: deal_out(jax.random.fold_in(streams_of[9], 2), own, number, TOK_DEV, EXPERTS, TOP, CAP, 2))(expert_ids_keys, expert_ids_turns).reshape((TOKENS, TOP))
    route_weights = jnp.clip(jnp.exp(math.log(1.0) - 2.9957323 * jax.random.uniform(streams_of[10], (TOKENS, TOP), jnp.float32) ** block_scale(streams_of[10], (TOKENS, TOP), ((0, 256),), -0.2, 0.2)), 0.05, 1.0)
    return {"residual": residual, "query_states": query_states, "key_states": key_states, "value_states": value_states, "out_proj": out_proj, "norm_gain": norm_gain, "w_gate": w_gate, "w_up": w_up, "w_down": w_down, "expert_ids": expert_ids, "route_weights": route_weights}


def folded_position(index):
    half_rows = TOK_CTX // 2
    shard = index // TOK_CTX
    within = index % TOK_CTX
    block = jnp.where(within < half_rows, shard, 2 * N_CTX - 1 - shard)
    return (block * half_rows + within % half_rows).astype(jnp.int32)

def reference(residual, query_states, key_states, value_states, out_proj, norm_gain, w_gate, w_up, w_down, expert_ids, route_weights):
    half_rows = TOK_CTX // 2
    group_size = HQ // KVH
    heads_dev = HQ // N_EP
    score_scale = 1.0 / math.sqrt(HD)
    positions = folded_position(jnp.arange(TOKENS, dtype=jnp.int32))
    blocks = TOKENS // half_rows

    def one_tile(number):
        block = number // HQ
        head = number % HQ
        query = lax.dynamic_slice(query_states, (block * half_rows, head * HD), (half_rows, HD))
        key_head = lax.dynamic_slice_in_dim(key_states, head // group_size * HD, HD, 1)
        value_head = lax.dynamic_slice_in_dim(value_states, head // group_size * HD, HD, 1)
        query_pos = lax.dynamic_slice_in_dim(positions, block * half_rows, half_rows)
        scores = jnp.dot(query, key_head.T, preferred_element_type=jnp.float32) * score_scale
        allowed = positions[None, :] <= query_pos[:, None]
        scores = jnp.where(allowed, scores, -1e+30)
        top_score = lax.optimization_barrier(jnp.max(scores, axis=1, keepdims=True))
        weights = jnp.where(allowed, jnp.exp(scores - top_score), 0.0)
        totals = lax.optimization_barrier(jnp.sum(weights, axis=1, keepdims=True))
        mixed = jnp.dot(weights.astype(jnp.bfloat16), value_head, preferred_element_type=jnp.float32)
        return (mixed / totals).astype(jnp.bfloat16)
    tiles = lax.map(one_tile, jnp.arange(blocks * HQ, dtype=jnp.int32))
    attended = tiles.reshape(blocks, HQ, half_rows, HD).transpose(0, 2, 1, 3).reshape(TOKENS, HQ * HD)

    def add_group(group, total):
        columns = lax.dynamic_slice_in_dim(attended, group * heads_dev * HD, heads_dev * HD, 1)
        rows_w = lax.dynamic_slice_in_dim(out_proj, group * heads_dev * HD, heads_dev * HD, 0)
        part = jnp.dot(columns, rows_w, preferred_element_type=jnp.float32).astype(jnp.bfloat16)
        part = lax.optimization_barrier(part)
        return total + part.astype(jnp.float32)
    projected = lax.fori_loop(0, N_EP, add_group, jnp.zeros((TOKENS, D), jnp.float32))
    stream = residual.astype(jnp.float32) + projected
    normed = (stream * lax.rsqrt(lax.optimization_barrier(jnp.mean(stream * stream, axis=1, keepdims=True)) + 1e-06) * norm_gain).astype(jnp.bfloat16)
    flat_ids = expert_ids.reshape(-1).astype(jnp.int32)
    flat_weights = route_weights.reshape(-1)
    order = jnp.argsort(flat_ids, stable=True).astype(jnp.int32)
    counts = jax.ops.segment_sum(jnp.ones_like(flat_ids), flat_ids, num_segments=EXPERTS).astype(jnp.int32)
    starts = (jnp.cumsum(counts) - counts).astype(jnp.int32)
    bound = CAP * (TOKENS // TOK_DEV)
    padded = jnp.concatenate([order, jnp.zeros((bound,), jnp.int32)])

    def one_expert(expert, mixture):
        picks = lax.dynamic_slice_in_dim(padded, starts[expert], bound)
        valid = jnp.arange(bound, dtype=jnp.int32) < counts[expert]
        token = (picks // TOP).astype(jnp.int32)
        weight = jnp.where(valid, flat_weights[picks], 0.0)
        rows = normed[token]
        halves = []
        for half in range(2):
            gate_acts = jnp.dot(rows, w_gate[2 * expert + half], preferred_element_type=jnp.float32)
            up_acts = jnp.dot(rows, w_up[2 * expert + half], preferred_element_type=jnp.float32)
            hidden = (jax.nn.silu(gate_acts) * up_acts).astype(jnp.bfloat16)
            halves.append(jnp.dot(hidden, w_down[2 * expert + half], preferred_element_type=jnp.float32).astype(jnp.bfloat16))
        expert_out = (halves[0].astype(jnp.float32) + halves[1].astype(jnp.float32)).astype(jnp.bfloat16)
        return mixture.at[token].add(weight[:, None] * expert_out.astype(jnp.float32))
    mixture = lax.fori_loop(0, EXPERTS, one_expert, jnp.zeros((TOKENS, D), jnp.float32))
    return (stream + mixture).astype(jnp.bfloat16)
```

```python
import functools
import math

import jax
import jax.numpy as jnp
from jax import lax
from jax.experimental import pallas as pl
from jax.experimental.pallas import tpu as pltpu
from jax.sharding import PartitionSpec as P

D = 2048
HD = 128
KVH = 4
HQ = 16
EXPERTS = 128
TOP = 8
CAP = 6
ROWS = 512
CORES = 2
BF = jnp.bfloat16
F32 = jnp.float32
LOG2_SCALE = math.log2(math.e) / math.sqrt(HD)


def attention_step(shards_in, first, last, *refs):
    ids_ref, q_ref = refs[0], refs[1]
    kv_refs = refs[2 : 2 + shards_in]
    rest = refs[2 + shards_in :]
    if first:
        m_in = l_in = a_in = None
    else:
        m_in, l_in, a_in = rest[:3]
        rest = rest[3:]
    if last:
        out_ref, m_ref, l_ref, a_ref = rest
    else:
        m_ref, l_ref, a_ref = rest
    own = ids_ref[0]
    if not first:
        m_ref[...] = m_in[...]
        l_ref[...] = l_in[...]
        a_ref[...] = a_in[...]

    def start_of(half):
        return half * ROWS if isinstance(half, int) else pl.multiple_of(half * ROWS, ROWS)

    def tile(slot, half, kv_ref, part, fresh, diagonal):
        query = q_ref[pl.ds(start_of(half), ROWS)]
        offset = start_of(part)
        key = kv_ref[pl.ds(offset, ROWS)]
        value = kv_ref[pl.ds(2 * ROWS + offset, ROWS)]
        scores = (
            lax.dot_general(key, query, (((1,), (1,)), ((), ())), preferred_element_type=F32)
            * LOG2_SCALE
        )
        if diagonal:
            key_at = lax.broadcasted_iota(jnp.int32, scores.shape, 0)
            query_at = lax.broadcasted_iota(jnp.int32, scores.shape, 1)
            scores = jnp.where(key_at <= query_at, scores, -1e30)
        top = jnp.max(scores, axis=0, keepdims=True)
        if not fresh:
            old = m_ref[slot]
            top = jnp.maximum(old, top)
            correction = jnp.exp2(old - top)
        weights = jnp.exp2(scores - top)
        total = jnp.sum(weights, axis=0, keepdims=True)
        mixed = lax.dot_general(
            value, weights.astype(BF), (((0,), (0,)), ((), ())), preferred_element_type=F32
        )
        if not fresh:
            total = l_ref[slot] * correction + total
            mixed = a_ref[slot] * correction + mixed
        m_ref[slot] = top
        l_ref[slot] = total
        a_ref[slot] = mixed

    for at in range(shards_in):
        if first and at == 0:
            tile(0, 0, kv_refs[0], 0, True, True)
            tile(1, 1, kv_refs[0], 1, True, True)
            tile(2, 1, kv_refs[0], 0, True, False)
            continue
        early = ids_ref[1 + at] < own
        half = jnp.where(early, 0, 1)
        tile(2, 1, kv_refs[at], 0, False, False)
        tile(half, half, kv_refs[at], jnp.where(early, 0, 1), False, False)
    if last:
        out_ref[0:ROWS] = (a_ref[0] / l_ref[0]).T.astype(BF)
        top = jnp.maximum(m_ref[1], m_ref[2])
        one = jnp.exp2(m_ref[1] - top)
        two = jnp.exp2(m_ref[2] - top)
        mixed = a_ref[1] * one + a_ref[2] * two
        out_ref[ROWS : 2 * ROWS] = (mixed / (l_ref[1] * one + l_ref[2] * two)).T.astype(BF)


def attend(ids, query, shards_kv, state, last):
    first = state is None
    count = len(shards_kv)
    vmem = pl.BlockSpec(memory_space=pltpu.VMEM)
    state_shapes = ((3, 1, ROWS), (3, 1, ROWS), (3, HD, ROWS))
    operands = [ids, query, *shards_kv] + ([] if first else list(state))
    if last:
        out_shape = jax.ShapeDtypeStruct(query.shape, BF)
        out_specs = vmem
        scratch = [pltpu.VMEM(shape, F32) for shape in state_shapes]
    else:
        out_shape = [jax.ShapeDtypeStruct(shape, F32) for shape in state_shapes]
        out_specs = [vmem] * 3
        scratch = []
    tiles = 2 * count + (1 if first else 0)
    return pl.pallas_call(
        functools.partial(attention_step, count, first, last),
        out_shape=out_shape,
        in_specs=[pl.BlockSpec(memory_space=pltpu.SMEM)] + [vmem] * (len(operands) - 1),
        out_specs=out_specs,
        scratch_shapes=scratch,
        compiler_params=pltpu.CompilerParams(vmem_limit_bytes=32 << 20),
        cost_estimate=pl.CostEstimate(
            flops=tiles * 4 * ROWS * ROWS * HD,
            bytes_accessed=count * 4 * ROWS * HD * 2 + 2 * ROWS * HD * 2,
            transcendentals=tiles * ROWS * ROWS,
        ),
    )(*operands)


def shards(
    residual,
    query_states,
    key_states,
    value_states,
    out_proj,
    norm_gain,
    w_gate,
    w_up,
    w_down,
    expert_ids,
    route_weights,
):
    n_ctx = lax.axis_size("ctx")
    n_ep = lax.axis_size("ep")
    planes = n_ctx // CORES
    tok = residual.shape[0]
    local_experts = EXPERTS // n_ctx
    ctx_index = lax.axis_index("ctx")
    ep_index = lax.axis_index("ep")
    plane, core = ctx_index // CORES, ctx_index % CORES
    kv_head = ep_index * KVH // n_ep
    far = planes // 2

    def z_perm(step):
        return [
            (z * CORES + c, ((z + step) % planes) * CORES + c)
            for z in range(planes)
            for c in range(CORES)
        ]

    up_perm, down_perm = z_perm(1), z_perm(-1)
    core_perm = [(i, i ^ 1) for i in range(n_ctx)]
    pair_perm = [(i, i ^ 1) for i in range(n_ep)]

    def up(x):
        return lax.ppermute(x, "ctx", up_perm)

    def down(x):
        return lax.ppermute(x, "ctx", down_perm)

    def across(x):
        return lax.ppermute(x, "ctx", core_perm)

    def ring(x):
        rows = x.shape[0] // 2
        blocks = [x]
        above = below = x
        for _ in range(far - 1):
            above, below = up(above), down(below)
            blocks += [above, below]
        blocks.append(jnp.concatenate([up(above[:rows]), down(below[rows:])], axis=0))
        return blocks

    offsets = [0]
    for step in range(1, far):
        offsets += [-step, step]
    offsets.append(far)

    def shard_id(offset, other):
        return ((plane + offset) % planes) * CORES + jnp.bitwise_xor(core, other)

    key_head = lax.dynamic_slice_in_dim(key_states, kv_head * HD, HD, 1)
    value_head = lax.dynamic_slice_in_dim(value_states, kv_head * HD, HD, 1)
    kv_blocks = ring(jnp.concatenate([key_head, value_head], axis=0))

    gates = (w_gate[0], lax.ppermute(w_gate[0], "ep", pair_perm))
    ups = (w_up[0], lax.ppermute(w_up[0], "ep", pair_perm))
    downs = (w_down[0], lax.ppermute(w_down[0], "ep", pair_perm))
    columns = D // CORES
    proj_mine = lax.all_gather(
        lax.dynamic_slice_in_dim(out_proj, core * columns, columns, 1), "ep", axis=0, tiled=True
    )
    proj_other = across(proj_mine)
    routing = lax.all_gather(
        jnp.concatenate([expert_ids.astype(F32), route_weights], axis=1), "ctx", axis=0
    )

    state = None
    groups = [[0]] + [[1 + 2 * s, 2 + 2 * s] for s in range(far - 1)] + [[2 * far - 1]]
    for number, group in enumerate(groups):
        held, ids = [], [ctx_index]
        for at in group:
            held += [kv_blocks[at], across(kv_blocks[at])]
            ids += [shard_id(offsets[at], 0), shard_id(offsets[at], 1)]
        state = attend(
            jnp.stack(ids).astype(jnp.int32), query_states, held, state, number == len(groups) - 1
        )
    attended = state

    heads = lax.all_to_all(
        attended.reshape(n_ep, tok, HD), "ep", split_axis=0, concat_axis=0, tiled=True
    )
    heads = heads.transpose(1, 0, 2).reshape(tok, HQ * HD)
    mine = jnp.dot(heads, proj_mine, preferred_element_type=F32)
    other = jnp.dot(heads, proj_other, preferred_element_type=F32)
    projected = jnp.where(
        core == 0,
        jnp.concatenate([mine, other], axis=1),
        jnp.concatenate([other, mine], axis=1),
    )
    stream = residual.astype(F32) + projected
    normed = (
        stream * lax.rsqrt(jnp.mean(stream * stream, axis=1, keepdims=True) + 1e-06) * norm_gain
    ).astype(BF)

    order = jnp.stack([shard_id(offset, other) for offset in offsets for other in range(CORES)])
    routing = jnp.take(routing, order, axis=0)
    ids = routing[:, :, :TOP].astype(jnp.int32)
    gains = routing[:, :, TOP:]
    experts = ctx_index * local_experts + jnp.arange(local_experts, dtype=jnp.int32)
    match = ids[:, :, :, None] == experts
    chosen = jnp.any(match, axis=2)
    weight = jnp.sum(jnp.where(match, gains[:, :, :, None], 0.0), axis=2)
    counts = chosen.astype(jnp.int32)
    rank = jnp.cumsum(counts, axis=1) - counts
    half = n_ctx // 2
    at_slot = jnp.logical_and(
        chosen[:, :, :, None], rank[:, :, :, None] == jnp.arange(CAP, dtype=jnp.int32)
    )
    placed = at_slot.reshape(2, half, tok, local_experts, CAP).transpose(0, 3, 1, 4, 2)
    same = jnp.eye(half, dtype=jnp.bool_)[None, None, :, None, :, None]
    select = jnp.where(same, placed[:, :, :, :, None, :], False)
    slots = local_experts * half * CAP
    scaled = weight.reshape(2, half, tok, local_experts).transpose(0, 3, 1, 2)
    spread = jnp.where(select, scaled[:, :, None, None, :, :], 0.0).reshape(2, slots, half * tok)
    select = select.reshape(2, slots, half * tok).astype(BF)
    spread_high = spread.astype(BF)
    spread_low = (spread - spread_high.astype(F32)).astype(BF)

    blocks = []
    for block in ring(normed):
        blocks += [block, across(block)]
    packed = [
        jnp.dot(
            select[h],
            jnp.concatenate(blocks[h * half : (h + 1) * half], axis=0),
            preferred_element_type=F32,
        )
        .astype(BF)
        .reshape(local_experts, half * CAP, D)
        for h in range(2)
    ]
    packed = jnp.stack(packed, axis=1).reshape(n_ep, half * CAP, D)
    arrived = lax.all_to_all(packed, "ep", split_axis=0, concat_axis=0, tiled=True)
    arrived = arrived.reshape(n_ep * half * CAP, D)
    halves = []
    for h in range(2):
        gate_acts = jnp.dot(arrived, gates[h], preferred_element_type=F32)
        up_acts = jnp.dot(arrived, ups[h], preferred_element_type=F32)
        hidden = (jax.nn.silu(gate_acts) * up_acts).astype(BF)
        halves.append(jnp.dot(hidden, downs[h], preferred_element_type=F32).astype(BF))
    expert_out = (halves[0].astype(F32) + halves[1].astype(F32)).astype(BF)
    returned = lax.all_to_all(
        expert_out.reshape(n_ep, half * CAP, D), "ep", split_axis=0, concat_axis=0, tiled=True
    ).reshape(local_experts, 2, half * CAP, D)

    def contract(table, rows):
        return lax.dot_general(table, rows, (((0,), (0,)), ((), ())), preferred_element_type=F32)

    shares = []
    for h in range(2):
        rows = returned[:, h].reshape(slots, D)
        share = contract(spread_high[h], rows) + contract(spread_low[h], rows)
        shares.append(share.reshape(half // CORES, CORES, tok, D))
    shares = jnp.concatenate(shares, axis=0).astype(BF)
    crossed = across(shares[:, 1])
    sums = shares[:, 0].astype(F32) + crossed.astype(F32)
    at = {offset: number for number, offset in enumerate(offsets)}
    cut = D // 2
    going_down = down(sums[at[far], :, :cut].astype(BF))
    going_up = up(sums[at[far], :, cut:].astype(BF))
    for step in range(far - 1, 0, -1):
        low, high = sums[at[-step]], sums[at[step]]
        if step == far - 1:
            low = jnp.concatenate([low[:, :cut] + going_down.astype(F32), low[:, cut:]], axis=1)
            high = jnp.concatenate([high[:, :cut], high[:, cut:] + going_up.astype(F32)], axis=1)
        else:
            low = low + going_down.astype(F32)
            high = high + going_up.astype(F32)
        going_down, going_up = down(low.astype(BF)), up(high.astype(BF))
    mixture = sums[at[0]] + going_down.astype(F32) + going_up.astype(F32)
    return (stream + mixture).astype(BF)


def solution(mesh):
    return jax.shard_map(
        shards,
        mesh=mesh,
        in_specs=(
            P(("ctx", "ep"), None),
            P("ctx", "ep"),
            P("ctx", None),
            P("ctx", None),
            P("ep", None),
            P(),
            P(("ctx", "ep"), None, None),
            P(("ctx", "ep"), None, None),
            P(("ctx", "ep"), None, None),
            P(("ctx", "ep"), None),
            P(("ctx", "ep"), None),
        ),
        out_specs=P(("ctx", "ep"), None),
        check_vma=False,
    )
```

```python
import functools
import math

import jax
import jax.numpy as jnp
from jax import lax
from jax.experimental import pallas as pl
from jax.experimental.pallas import tpu as pltpu
from jax.sharding import PartitionSpec as P

D = 2048
HD = 128
KVH = 4
HQ = 16
EXPERTS = 128
TOP = 8
CAP = 6
ROWS = 512
CORES = 2
BF = jnp.bfloat16
F32 = jnp.float32
TABLE = 32
NO_COST = pl.CostEstimate(flops=0, bytes_accessed=0, transcendentals=0)
LOG2_SCALE = math.log2(math.e) / math.sqrt(HD)


def attention_step(shards_in, split, diagonal, fresh, last, *refs):
    ids_ref, q_ref = refs[0], refs[1]
    if split:
        kv_refs = [(refs[2], refs[3], 0)]
        rest = refs[4:]
    else:
        kv_refs = [(ref, ref, 2 * ROWS) for ref in refs[2 : 2 + shards_in]]
        rest = refs[2 + shards_in :]
    if not fresh:
        m_in, l_in, a_in = rest[:3]
        rest = rest[3:]
    if last:
        out_ref, m_ref, l_ref, a_ref = rest
    else:
        m_ref, l_ref, a_ref = rest
    own = ids_ref[0]
    if not fresh:
        m_ref[...] = m_in[...]
        l_ref[...] = l_in[...]
        a_ref[...] = a_in[...]
    elif not diagonal:
        m_ref[...] = jnp.full(m_ref.shape, -1e30, F32)
        l_ref[...] = jnp.zeros(l_ref.shape, F32)
        a_ref[...] = jnp.zeros(a_ref.shape, F32)

    def start_of(half):
        return half * ROWS if isinstance(half, int) else pl.multiple_of(half * ROWS, ROWS)

    def tile(slot, half, kv, part, new, masked):
        key_ref, value_ref, values_at = kv
        query = q_ref[pl.ds(start_of(half), ROWS)]
        offset = start_of(part)
        key = key_ref[pl.ds(offset, ROWS)]
        value = value_ref[pl.ds(values_at + offset, ROWS)]
        scores = (
            lax.dot_general(key, query, (((1,), (1,)), ((), ())), preferred_element_type=F32)
            * LOG2_SCALE
        )
        if masked:
            key_at = lax.broadcasted_iota(jnp.int32, scores.shape, 0)
            query_at = lax.broadcasted_iota(jnp.int32, scores.shape, 1)
            scores = jnp.where(key_at <= query_at, scores, -1e30)
        top = jnp.max(scores, axis=0, keepdims=True)
        if not new:
            old = m_ref[slot]
            top = jnp.maximum(old, top)
            correction = jnp.exp2(old - top)
        weights = jnp.exp2(scores - top)
        total = jnp.sum(weights, axis=0, keepdims=True)
        mixed = lax.dot_general(
            value, weights.astype(BF), (((0,), (0,)), ((), ())), preferred_element_type=F32
        )
        if not new:
            total = l_ref[slot] * correction + total
            mixed = a_ref[slot] * correction + mixed
        m_ref[slot] = top
        l_ref[slot] = total
        a_ref[slot] = mixed

    for at in range(shards_in):
        if diagonal:
            tile(0, 0, kv_refs[0], 0, True, True)
            tile(1, 1, kv_refs[0], 1, True, True)
            tile(2, 1, kv_refs[0], 0, True, False)
            continue
        early = ids_ref[1 + at] < own
        half = jnp.where(early, 0, 1)
        tile(2, 1, kv_refs[at], 0, False, False)
        tile(half, half, kv_refs[at], jnp.where(early, 0, 1), False, False)
    if last:
        top = jnp.maximum(m_ref[1], m_ref[2])
        one = jnp.exp2(m_ref[1] - top)
        two = jnp.exp2(m_ref[2] - top)
        out_ref[0, 0:HD] = a_ref[0]
        out_ref[0, HD : HD + 8] = jnp.broadcast_to(m_ref[0], (8, ROWS))
        out_ref[0, HD + 8 : HD + 16] = jnp.broadcast_to(l_ref[0], (8, ROWS))
        out_ref[1, 0:HD] = a_ref[1] * one + a_ref[2] * two
        out_ref[1, HD : HD + 8] = jnp.broadcast_to(top, (8, ROWS))
        out_ref[1, HD + 8 : HD + 16] = jnp.broadcast_to(
            l_ref[1] * one + l_ref[2] * two, (8, ROWS)
        )


def attend(ids, query, shards_kv, state, diagonal=False, split=False, last=False):
    fresh = state is None
    count = 1 if split else len(shards_kv)
    vmem = pl.BlockSpec(memory_space=pltpu.VMEM)
    state_shapes = ((3, 1, ROWS), (3, 1, ROWS), (3, HD, ROWS))
    operands = [ids, query, *shards_kv] + ([] if fresh else list(state))
    if last:
        out_shape = jax.ShapeDtypeStruct((2, HD + 16, ROWS), F32)
        out_specs = vmem
        scratch = [pltpu.VMEM(shape, F32) for shape in state_shapes]
    else:
        out_shape = [jax.ShapeDtypeStruct(shape, F32) for shape in state_shapes]
        out_specs = [vmem] * 3
        scratch = []
    return pl.pallas_call(
        functools.partial(attention_step, count, split, diagonal, fresh, last),
        out_shape=out_shape,
        in_specs=[pl.BlockSpec(memory_space=pltpu.SMEM)] + [vmem] * (len(operands) - 1),
        out_specs=out_specs,
        scratch_shapes=scratch,
        compiler_params=pltpu.CompilerParams(vmem_limit_bytes=32 << 20),
        cost_estimate=NO_COST,
    )(*operands)


def merge_kernel(one_ref, two_ref, out_ref):
    for half in range(2):
        top_one, top_two = one_ref[half, HD : HD + 1], two_ref[half, HD : HD + 1]
        top = jnp.maximum(top_one, top_two)
        one, two = jnp.exp2(top_one - top), jnp.exp2(top_two - top)
        total = one_ref[half, HD + 8 : HD + 9] * one + two_ref[half, HD + 8 : HD + 9] * two
        mixed = one_ref[half, 0:HD] * one + two_ref[half, 0:HD] * two
        rows = (mixed / total).T.astype(BF)
        out_ref[half * ROWS : (half + 1) * ROWS] = rows


def merge(one, two):
    vmem = pl.BlockSpec(memory_space=pltpu.VMEM)
    return pl.pallas_call(
        merge_kernel,
        out_shape=jax.ShapeDtypeStruct((2 * ROWS, HD), BF),
        in_specs=[vmem, vmem],
        out_specs=vmem,
        compiler_params=pltpu.CompilerParams(vmem_limit_bytes=32 << 20),
        cost_estimate=NO_COST,
    )(one, two)


def stage_kernel(head_ref, key_ref, value_ref, ids_ref, gain_ref, out_ref):
    rows = key_ref.shape[0]
    out_ref[0:rows] = key_ref[...]
    out_ref[rows : 2 * rows] = value_ref[...]
    gains = gain_ref[...]
    high = gains.astype(BF)
    low = (gains - high.astype(F32)).astype(BF)
    tok = gains.shape[0]
    at = lax.broadcasted_iota(jnp.int32, (tok, HD), 0)
    to = lax.broadcasted_iota(jnp.int32, (tok, HD), 1)
    eye = (at == to).astype(F32).astype(BF)

    def turned(part):
        return lax.dot_general(part, eye, (((0,), (0,)), ((), ())), preferred_element_type=F32)

    ids = ids_ref[...].astype(F32).astype(BF)
    table = [turned(part) for part in (ids, high, low)]
    table.append(jnp.zeros((TABLE - 3 * TOP, HD), F32))
    out_ref[2 * rows : 2 * rows + TABLE] = jnp.concatenate(table, axis=0).astype(BF)


def stage(head, keys, values, ids, gains):
    rows, tok = keys.shape[0], ids.shape[0]
    column = pl.BlockSpec((rows, HD), lambda i, head: (0, head[0]))
    small = pl.BlockSpec((tok, TOP), lambda i, head: (0, 0))
    return pl.pallas_call(
        stage_kernel,
        grid_spec=pltpu.PrefetchScalarGridSpec(
            num_scalar_prefetch=1,
            grid=(1,),
            in_specs=[column, column, small, small],
            out_specs=pl.BlockSpec((2 * rows + TABLE, HD), lambda i, head: (0, 0)),
        ),
        out_shape=jax.ShapeDtypeStruct((2 * rows + TABLE, HD), BF),
        compiler_params=pltpu.CompilerParams(vmem_limit_bytes=32 << 20),
        cost_estimate=NO_COST,
    )(head, keys, values, ids, gains)


def route_kernel(tok, local, ctx_ref, *refs):
    tables, (select_ref, high_ref, low_ref) = refs[:-3], refs[-3:]
    shards_in = len(tables)
    held = [table[...].astype(F32)[:, :tok] for table in tables]
    table = jnp.concatenate(held, axis=1)
    width = shards_in * tok
    own = ctx_ref[0]
    turn = lax.broadcasted_iota(jnp.int32, (CORES * local, width), 0)
    first = jnp.where(turn < local, own * local, (own + 1 - 2 * (own % 2)) * local - local)
    expert = (first + turn).astype(F32)
    chosen = jnp.zeros((CORES * local, width), F32)
    high = jnp.zeros((CORES * local, width), F32)
    low = jnp.zeros((CORES * local, width), F32)
    for k in range(TOP):
        hit = table[k : k + 1] == expert
        chosen = chosen + jnp.where(hit, 1.0, 0.0)
        high = high + jnp.where(hit, table[TOP + k : TOP + k + 1], 0.0)
        low = low + jnp.where(hit, table[2 * TOP + k : 2 * TOP + k + 1], 0.0)
    before = lax.broadcasted_iota(jnp.int32, (width, width), 0)
    after = lax.broadcasted_iota(jnp.int32, (width, width), 1)
    earlier = jnp.logical_and(before // tok == after // tok, before < after)
    rank = jnp.dot(
        chosen.astype(BF), earlier.astype(F32).astype(BF), preferred_element_type=F32
    )
    shard = lax.broadcasted_iota(jnp.int32, (CORES * local, width), 1) // tok
    slot = jnp.where(chosen > 0.5, rank + (shard * CAP).astype(F32), -1.0)
    column = shards_in * CAP
    row = lax.broadcasted_iota(jnp.int32, (column, width), 0).astype(F32)
    for number in range(CORES * local):
        at = slice(number % local * column, (number % local + 1) * column)
        here = row == slot[number : number + 1]
        group = number // local
        select_ref[group, at] = jnp.where(here, 1.0, 0.0).astype(BF)
        high_ref[group, at] = jnp.where(here, high[number : number + 1], 0.0).astype(BF)
        low_ref[group, at] = jnp.where(here, low[number : number + 1], 0.0).astype(BF)


def route(ctx, tables, tok, local):
    slots, width = local * len(tables) * CAP, len(tables) * tok
    shape = (CORES, slots, width)
    in_specs = [
        pl.BlockSpec(
            (TABLE, HD), functools.partial(lambda last, i, ctx: (last, 0), table.shape[0] // TABLE - 1)
        )
        for table in tables
    ]
    return pl.pallas_call(
        functools.partial(route_kernel, tok, local),
        grid_spec=pltpu.PrefetchScalarGridSpec(
            num_scalar_prefetch=1,
            grid=(1,),
            in_specs=in_specs,
            out_specs=[pl.BlockSpec(shape, lambda i, ctx: (0, 0, 0))] * 3,
        ),
        out_shape=[jax.ShapeDtypeStruct(shape, BF)] * 3,
        compiler_params=pltpu.CompilerParams(vmem_limit_bytes=32 << 20),
        cost_estimate=NO_COST,
    )(ctx, *tables)


def project_kernel(*refs):
    heads, proj, out_ref = refs[:4], refs[4:8], refs[8]
    total = None
    for pair in ((0, 1), (2, 3)):
        rows = jnp.concatenate([heads[at][...] for at in pair], axis=1)
        table = jnp.concatenate([proj[at][...] for at in pair], axis=0)
        part = jnp.dot(rows, table, preferred_element_type=F32)
        total = part if total is None else total + part
    out_ref[...] = total.astype(BF)


def project(heads, proj):
    vmem = pl.BlockSpec(memory_space=pltpu.VMEM)
    return pl.pallas_call(
        project_kernel,
        out_shape=jax.ShapeDtypeStruct((heads[0].shape[0], D), BF),
        in_specs=[vmem] * 8,
        out_specs=vmem,
        compiler_params=pltpu.CompilerParams(vmem_limit_bytes=32 << 20),
        cost_estimate=NO_COST,
    )(*heads, *proj)


BLOCK = 384


def expert_kernel(rows_ref, gate_ref, up_ref, down_ref, *refs):
    other_gate, other_up, other_down, out_ref = refs

    def half(rows, gate, up):
        gate_acts = jnp.dot(rows, gate[0], preferred_element_type=F32)
        up_acts = jnp.dot(rows, up[0], preferred_element_type=F32)
        return (gate_acts / (1.0 + jnp.exp(-gate_acts)) * up_acts).astype(BF)

    def block(number, carry):
        at = pl.ds(pl.multiple_of(number * BLOCK, BLOCK), BLOCK)
        rows = rows_ref[at]
        own = half(rows, gate_ref, up_ref)
        other = half(rows, other_gate, other_up)
        one = jnp.dot(own, down_ref[0], preferred_element_type=F32).astype(BF)
        two = jnp.dot(other, other_down[0], preferred_element_type=F32).astype(BF)
        out_ref[at] = (one.astype(F32) + two.astype(F32)).astype(BF)
        return carry

    lax.fori_loop(0, rows_ref.shape[0] // BLOCK, block, 0)


def experts_apply(rows, gate, up, down, swapped):
    vmem = pl.BlockSpec(memory_space=pltpu.VMEM)
    return pl.pallas_call(
        expert_kernel,
        out_shape=jax.ShapeDtypeStruct(rows.shape, BF),
        in_specs=[vmem] * 7,
        out_specs=vmem,
        compiler_params=pltpu.CompilerParams(vmem_limit_bytes=32 << 20),
        cost_estimate=pl.CostEstimate(
            flops=12 * rows.shape[0] * D * gate.shape[2],
            bytes_accessed=12 * D * gate.shape[2] + 4 * rows.shape[0] * D,
            transcendentals=2 * rows.shape[0] * gate.shape[2],
        ),
    )(rows, gate, up, down, *swapped)


def shards(
    residual,
    query_states,
    key_states,
    value_states,
    out_proj,
    norm_gain,
    w_gate,
    w_up,
    w_down,
    expert_ids,
    route_weights,
):
    n_ctx = lax.axis_size("ctx")
    n_ep = lax.axis_size("ep")
    planes = n_ctx // CORES
    tok = residual.shape[0]
    local_experts = EXPERTS // n_ctx
    ctx_index = lax.axis_index("ctx")
    ep_index = lax.axis_index("ep")
    plane, core = ctx_index // CORES, ctx_index % CORES
    kv_head = ep_index * KVH // n_ep
    far = planes // 2
    side = 4
    turn_x, turn_y = ep_index // side, ep_index % side

    def z_perm(step):
        return [
            (z * CORES + c, ((z + step) % planes) * CORES + c)
            for z in range(planes)
            for c in range(CORES)
        ]

    up_perm, down_perm = z_perm(1), z_perm(-1)
    core_perm = [(i, i ^ 1) for i in range(n_ctx)]
    pair_perm = [(i, i ^ 1) for i in range(n_ep)]
    y_perms = [
        [(x * side + y, x * side + (y + step) % side) for x in range(side) for y in range(side)]
        for step in (1, -1)
    ]
    x_perms = [
        [(x * side + y, (x + step) % side * side + y) for x in range(side) for y in range(side)]
        for step in (1, -1)
    ]

    def up(x):
        return lax.ppermute(x, "ctx", up_perm)

    def down(x):
        return lax.ppermute(x, "ctx", down_perm)

    def across(x):
        return lax.ppermute(x, "ctx", core_perm)

    def swap(x):
        return lax.ppermute(x, "ep", pair_perm)

    tie = lax.optimization_barrier

    offsets = [0]
    for step in range(1, far):
        offsets += [-step, step]
    offsets.append(far)

    def shard_id(offset, other):
        return ((plane + offset) % planes) * CORES + jnp.bitwise_xor(core, other)

    key_rows = key_states.shape[0]
    kv_own = stage(
        kv_head.astype(jnp.int32).reshape(1), key_states, value_states, expert_ids, route_weights
    )

    def ids_of(other, offs):
        ids = [jnp.bitwise_xor(ctx_index, other)] + [shard_id(o, 0) for o in offs]
        return jnp.stack(ids).astype(jnp.int32)

    query_other = across(query_states)
    queries = (query_states, query_other)
    tables = [kv_own]
    states = [None, None]
    above, below = up(kv_own), down(kv_own)
    gate_other = swap(w_gate)
    two_y = [(x * side + y, x * side + (y + 2) % side) for x in range(side) for y in range(side)]
    two_x = [(x * side + y, (x + 2) % side * side + y) for x in range(side) for y in range(side)]
    proj = [out_proj] + [lax.ppermute(out_proj, "ep", perm) for perm in (*x_perms, two_x)]
    states[0] = attend(ids_of(0, []), queries[0], [kv_own], None, diagonal=True)
    states[1] = attend(ids_of(1, [0]), queries[1], [kv_own], None)
    for step in range(1, far):
        above, below, states = tie((above, below, states))
        held = [above, below]
        tables += held
        if step < far - 1:
            above, below = up(above), down(below)
        else:
            last_top, last_low = up(above[:key_rows]), down(below[key_rows:])
        states[0] = attend(ids_of(0, [-step, step]), queries[0], held, states[0])
        states[1] = attend(ids_of(1, [-step, step]), queries[1], held, states[1])
    last_top, last_low, states, gate_other, proj = tie(
        (last_top, last_low, states, gate_other, proj)
    )
    up_other = swap(tie((w_up, last_low))[0])
    held = [last_top, last_low]
    tables.append(last_low)
    part_other = attend(ids_of(1, [far]), queries[1], held, states[1], split=True, last=True)
    part_joined = across(part_other)
    part_own = attend(ids_of(0, [far]), queries[0], held, states[0], split=True, last=True)
    attended = merge(part_own, part_joined).reshape(side, side * tok, HD)

    def x_chunk(step):
        return lax.dynamic_index_in_dim(attended, (turn_x + step) % side, 0, keepdims=False)

    heads = [
        x_chunk(0),
        lax.ppermute(x_chunk(1), "ep", x_perms[0]),
        lax.ppermute(x_chunk(-1), "ep", x_perms[1]),
        lax.ppermute(x_chunk(2), "ep", two_x),
    ]
    partial = project(heads, proj).reshape(side, tok, D)
    partial, up_other = tie((partial, up_other))

    def y_chunk(step):
        return lax.dynamic_index_in_dim(partial, (turn_y + step) % side, 0, keepdims=False)

    projected = y_chunk(0).astype(F32)
    for step, perm in ((2, two_y), (1, y_perms[0]), (-1, y_perms[1])):
        projected = projected + lax.ppermute(y_chunk(step), "ep", perm).astype(F32)
    stream = residual.astype(F32) + projected
    normed = (
        stream * lax.rsqrt(jnp.mean(stream * stream, axis=1, keepdims=True) + 1e-06) * norm_gain
    ).astype(BF)

    down_other = swap(tie((w_down, normed))[0])

    select, spread_high, spread_low = route(
        ctx_index.astype(jnp.int32).reshape(1), tables, tok, local_experts
    )
    column = planes * CAP
    slots = local_experts * column

    blocks = [normed]
    above = below = normed
    for step in range(1, far):
        above, below = up(above), down(below)
        blocks += [above, below]
    rows = tok // 2
    last_top, last_low = up(above[:rows]), down(below[rows:])
    last_top, last_low, down_other = tie((last_top, last_low, down_other))
    blocks += [last_top, last_low]
    gathered = jnp.concatenate(blocks, axis=0)

    def pack(which, gathered):
        return (
            jnp.dot(select[which], gathered, preferred_element_type=F32)
            .astype(BF)
            .reshape(local_experts, column, D)
        )

    def exchange(rows):
        return lax.all_to_all(
            rows.reshape(n_ep, slots // n_ep, D), "ep", split_axis=0, concat_axis=0, tiled=True
        ).reshape(slots, D)

    packed, gathered = tie((pack(0, gathered), gathered))
    arrived = exchange(packed)
    crossing = across(pack(1, gathered))
    arrived_other = exchange(tie((crossing, arrived))[0])
    swapped = (gate_other, up_other, down_other)
    out = experts_apply(arrived, w_gate, w_up, w_down, swapped)
    returned = exchange(out)
    out_other = experts_apply(arrived_other, w_gate, w_up, w_down, swapped)
    returned_other = across(exchange(out_other))

    def contract(table, rows):
        return lax.dot_general(table, rows, (((0,), (0,)), ((), ())), preferred_element_type=F32)

    sums = contract(spread_high[0], returned) + contract(spread_low[0], returned)
    sums = sums + contract(spread_high[1], returned_other)
    sums = sums + contract(spread_low[1], returned_other)
    sums = sums.reshape(planes, tok, D)
    at = {offset: number for number, offset in enumerate(offsets)}
    cut = D // 2
    going_down = down(sums[at[far], :, :cut].astype(BF))
    going_up = up(sums[at[far], :, cut:].astype(BF))
    for step in range(far - 1, 0, -1):
        low, high = sums[at[-step]], sums[at[step]]
        if step == far - 1:
            low = jnp.concatenate([low[:, :cut] + going_down.astype(F32), low[:, cut:]], axis=1)
            high = jnp.concatenate([high[:, :cut], high[:, cut:] + going_up.astype(F32)], axis=1)
        else:
            low = low + going_down.astype(F32)
            high = high + going_up.astype(F32)
        going_down, going_up = down(low.astype(BF)), up(high.astype(BF))
    mixture = sums[at[0]] + going_down.astype(F32) + going_up.astype(F32)
    return (stream + mixture).astype(BF)


def solution(mesh):
    return jax.shard_map(
        shards,
        mesh=mesh,
        in_specs=(
            P(("ctx", "ep"), None),
            P("ctx", "ep"),
            P("ctx", None),
            P("ctx", None),
            P("ep", None),
            P(),
            P(("ctx", "ep"), None, None),
            P(("ctx", "ep"), None, None),
            P(("ctx", "ep"), None, None),
            P(("ctx", "ep"), None),
            P(("ctx", "ep"), None),
        ),
        out_specs=P(("ctx", "ep"), None),
        check_vma=False,
    )
```

```python
import functools
import math

import jax
import jax.numpy as jnp
from jax import lax
from jax.experimental import pallas as pl
from jax.experimental.pallas import tpu as pltpu
from jax.sharding import PartitionSpec as P

D = 2048
HD = 128
KVH = 4
HQ = 16
EXPERTS = 128
TOP = 8
CAP = 6
ROWS = 512
CORES = 2
BF = jnp.bfloat16
F32 = jnp.float32
TABLE = 32
NO_COST = pl.CostEstimate(flops=0, bytes_accessed=0, transcendentals=0)
LOG2_SCALE = math.log2(math.e) / math.sqrt(HD)


def attention_step(shards_in, split, diagonal, fresh, last, *refs):
    ids_ref, q_ref = refs[0], refs[1]
    if split:
        kv_refs = [(refs[2], refs[3], 0)]
        rest = refs[4:]
    else:
        kv_refs = [(ref, ref, 2 * ROWS) for ref in refs[2 : 2 + shards_in]]
        rest = refs[2 + shards_in :]
    if not fresh:
        m_in, l_in, a_in = rest[:3]
        rest = rest[3:]
    if last:
        out_ref, m_ref, l_ref, a_ref = rest
    else:
        m_ref, l_ref, a_ref = rest
    own = ids_ref[0]
    if not fresh:
        m_ref[...] = m_in[...]
        l_ref[...] = l_in[...]
        a_ref[...] = a_in[...]
    elif not diagonal:
        m_ref[...] = jnp.full(m_ref.shape, -1e30, F32)
        l_ref[...] = jnp.zeros(l_ref.shape, F32)
        a_ref[...] = jnp.zeros(a_ref.shape, F32)

    def start_of(half):
        return half * ROWS if isinstance(half, int) else pl.multiple_of(half * ROWS, ROWS)

    def tile(slot, half, kv, part, new, masked):
        key_ref, value_ref, values_at = kv
        query = q_ref[pl.ds(start_of(half), ROWS)]
        offset = start_of(part)
        key = key_ref[pl.ds(offset, ROWS)]
        value = value_ref[pl.ds(values_at + offset, ROWS)]
        scores = (
            lax.dot_general(key, query, (((1,), (1,)), ((), ())), preferred_element_type=F32)
            * LOG2_SCALE
        )
        if masked:
            key_at = lax.broadcasted_iota(jnp.int32, scores.shape, 0)
            query_at = lax.broadcasted_iota(jnp.int32, scores.shape, 1)
            scores = jnp.where(key_at <= query_at, scores, -1e30)
        top = jnp.max(scores, axis=0, keepdims=True)
        if not new:
            old = m_ref[slot]
            top = jnp.maximum(old, top)
            correction = jnp.exp2(old - top)
        weights = jnp.exp2(scores - top)
        total = jnp.sum(weights, axis=0, keepdims=True)
        mixed = lax.dot_general(
            value, weights.astype(BF), (((0,), (0,)), ((), ())), preferred_element_type=F32
        )
        if not new:
            total = l_ref[slot] * correction + total
            mixed = a_ref[slot] * correction + mixed
        m_ref[slot] = top
        l_ref[slot] = total
        a_ref[slot] = mixed

    for at in range(shards_in):
        if diagonal:
            tile(0, 0, kv_refs[0], 0, True, True)
            tile(1, 1, kv_refs[0], 1, True, True)
            tile(2, 1, kv_refs[0], 0, True, False)
            continue
        early = ids_ref[1 + at] < own
        half = jnp.where(early, 0, 1)
        tile(2, 1, kv_refs[at], 0, False, False)
        tile(half, half, kv_refs[at], jnp.where(early, 0, 1), False, False)
    if last:
        top = jnp.maximum(m_ref[1], m_ref[2])
        one = jnp.exp2(m_ref[1] - top)
        two = jnp.exp2(m_ref[2] - top)
        out_ref[0, 0:HD] = a_ref[0]
        out_ref[0, HD : HD + 8] = jnp.broadcast_to(m_ref[0], (8, ROWS))
        out_ref[0, HD + 8 : HD + 16] = jnp.broadcast_to(l_ref[0], (8, ROWS))
        out_ref[1, 0:HD] = a_ref[1] * one + a_ref[2] * two
        out_ref[1, HD : HD + 8] = jnp.broadcast_to(top, (8, ROWS))
        out_ref[1, HD + 8 : HD + 16] = jnp.broadcast_to(
            l_ref[1] * one + l_ref[2] * two, (8, ROWS)
        )


def attend(ids, query, shards_kv, state, diagonal=False, split=False, last=False):
    fresh = state is None
    count = 1 if split else len(shards_kv)
    vmem = pl.BlockSpec(memory_space=pltpu.VMEM)
    state_shapes = ((3, 1, ROWS), (3, 1, ROWS), (3, HD, ROWS))
    operands = [ids, query, *shards_kv] + ([] if fresh else list(state))
    if last:
        out_shape = jax.ShapeDtypeStruct((2, HD + 16, ROWS), F32)
        out_specs = vmem
        scratch = [pltpu.VMEM(shape, F32) for shape in state_shapes]
    else:
        out_shape = [jax.ShapeDtypeStruct(shape, F32) for shape in state_shapes]
        out_specs = [vmem] * 3
        scratch = []
    return pl.pallas_call(
        functools.partial(attention_step, count, split, diagonal, fresh, last),
        out_shape=out_shape,
        in_specs=[pl.BlockSpec(memory_space=pltpu.SMEM)] + [vmem] * (len(operands) - 1),
        out_specs=out_specs,
        scratch_shapes=scratch,
        compiler_params=pltpu.CompilerParams(vmem_limit_bytes=16 << 20),
        cost_estimate=pl.CostEstimate(
            flops=24 * count * ROWS * ROWS * HD, bytes_accessed=0, transcendentals=0
        ),
    )(*operands)


def merge_kernel(one_ref, two_ref, out_ref):
    for half in range(2):
        top_one, top_two = one_ref[half, HD : HD + 1], two_ref[half, HD : HD + 1]
        top = jnp.maximum(top_one, top_two)
        one, two = jnp.exp2(top_one - top), jnp.exp2(top_two - top)
        total = one_ref[half, HD + 8 : HD + 9] * one + two_ref[half, HD + 8 : HD + 9] * two
        mixed = one_ref[half, 0:HD] * one + two_ref[half, 0:HD] * two
        rows = (mixed / total).T.astype(BF)
        out_ref[half * ROWS : (half + 1) * ROWS] = rows


def merge(one, two):
    vmem = pl.BlockSpec(memory_space=pltpu.VMEM)
    return pl.pallas_call(
        merge_kernel,
        out_shape=jax.ShapeDtypeStruct((2 * ROWS, HD), BF),
        in_specs=[vmem, vmem],
        out_specs=vmem,
        compiler_params=pltpu.CompilerParams(vmem_limit_bytes=16 << 20),
        cost_estimate=NO_COST,
    )(one, two)


def stage_kernel(head_ref, key_ref, value_ref, ids_ref, gain_ref, out_ref):
    rows = key_ref.shape[0]
    out_ref[0:rows] = key_ref[...]
    out_ref[rows : 2 * rows] = value_ref[...]
    tok = ids_ref.shape[1]
    table = jnp.concatenate([ids_ref[...].astype(F32), gain_ref[...]], axis=0)
    out_ref[2 * rows : 2 * rows + TABLE] = jnp.concatenate(
        [
            jnp.concatenate([table, jnp.zeros((TABLE - 2 * TOP, tok), F32)], axis=0),
            jnp.zeros((TABLE, HD - tok), F32),
        ],
        axis=1,
    ).astype(BF)


def stage(head, keys, values, ids, gains):
    rows, tok = keys.shape[0], ids.shape[1]
    column = pl.BlockSpec((rows, HD), lambda i, head: (0, head[0]))
    small = pl.BlockSpec((TOP, tok), lambda i, head: (0, 0))
    return pl.pallas_call(
        stage_kernel,
        grid_spec=pltpu.PrefetchScalarGridSpec(
            num_scalar_prefetch=1,
            grid=(1,),
            in_specs=[column, column, small, small],
            out_specs=pl.BlockSpec((2 * rows + TABLE, HD), lambda i, head: (0, 0)),
        ),
        out_shape=jax.ShapeDtypeStruct((2 * rows + TABLE, HD), BF),
        compiler_params=pltpu.CompilerParams(vmem_limit_bytes=60 << 20),
        cost_estimate=NO_COST,
    )(head, keys, values, ids, gains)


def route_kernel(tok, local, ctx_ref, *refs):
    tables, (select_ref, spread_ref) = refs[:-2], refs[-2:]
    shards_in = len(tables)
    held = [table[...].astype(F32)[:, :tok] for table in tables]
    table = jnp.concatenate(held, axis=1)
    width = shards_in * tok
    own = ctx_ref[0]
    turn = lax.broadcasted_iota(jnp.int32, (CORES * local, width), 0)
    first = jnp.where(turn < local, own * local, (own + 1 - 2 * (own % 2)) * local - local)
    expert = (first + turn).astype(F32)
    chosen = jnp.zeros((CORES * local, width), F32)
    weight = jnp.zeros((CORES * local, width), F32)
    for k in range(TOP):
        hit = table[k : k + 1] == expert
        chosen = chosen + jnp.where(hit, 1.0, 0.0)
        weight = weight + jnp.where(hit, table[TOP + k : TOP + k + 1], 0.0)
    before = lax.broadcasted_iota(jnp.int32, (width, width), 0)
    after = lax.broadcasted_iota(jnp.int32, (width, width), 1)
    earlier = jnp.logical_and(before // tok == after // tok, before < after)
    rank = jnp.dot(
        chosen.astype(BF), earlier.astype(F32).astype(BF), preferred_element_type=F32
    )
    shard = lax.broadcasted_iota(jnp.int32, (CORES * local, width), 1) // tok
    slot = jnp.where(chosen > 0.5, rank + (shard * CAP).astype(F32), -1.0)
    column = shards_in * CAP
    row = lax.broadcasted_iota(jnp.int32, (column, width), 0).astype(F32)
    for number in range(CORES * local):
        at = slice(number % local * column, (number % local + 1) * column)
        here = row == slot[number : number + 1]
        group = number // local
        select_ref[group, at] = jnp.where(here, 1.0, 0.0).astype(BF)
        spread_ref[group, at] = jnp.where(here, weight[number : number + 1], 0.0).astype(BF)


def route(ctx, tables, tok, local):
    slots, width = local * len(tables) * CAP, len(tables) * tok
    shape = (CORES, slots, width)
    in_specs = [
        pl.BlockSpec(
            (TABLE, HD), functools.partial(lambda last, i, ctx: (last, 0), table.shape[0] // TABLE - 1)
        )
        for table in tables
    ]
    return pl.pallas_call(
        functools.partial(route_kernel, tok, local),
        grid_spec=pltpu.PrefetchScalarGridSpec(
            num_scalar_prefetch=1,
            grid=(1,),
            in_specs=in_specs,
            out_specs=[pl.BlockSpec(shape, lambda i, ctx: (0, 0, 0))] * 2,
        ),
        out_shape=[jax.ShapeDtypeStruct(shape, BF)] * 2,
        compiler_params=pltpu.CompilerParams(vmem_limit_bytes=32 << 20),
        cost_estimate=NO_COST,
    )(ctx, *tables)


def project_kernel(*refs):
    heads, proj, out_ref = refs[:4], refs[4:9], refs[9]
    tables = [proj[0][...], proj[1][...], proj[2][...]]
    tables.append(jnp.concatenate([proj[3][...], proj[4][...]], axis=0))
    total = None
    for pair in ((0, 1), (2, 3)):
        rows = jnp.concatenate([heads[at][...] for at in pair], axis=1)
        table = jnp.concatenate([tables[at] for at in pair], axis=0)
        part = jnp.dot(rows, table, preferred_element_type=F32)
        total = part if total is None else total + part
    out_ref[...] = total.astype(BF)


def project(heads, proj):
    vmem = pl.BlockSpec(memory_space=pltpu.VMEM)
    return pl.pallas_call(
        project_kernel,
        out_shape=jax.ShapeDtypeStruct((heads[0].shape[0], D), BF),
        in_specs=[vmem] * 9,
        out_specs=vmem,
        compiler_params=pltpu.CompilerParams(vmem_limit_bytes=60 << 20),
        cost_estimate=NO_COST,
    )(*heads, *proj)


BLOCK = 384


def expert_kernel(rows_ref, gate_ref, up_ref, down_ref, *refs):
    other_gate, other_up, down_top, down_low, out_ref = refs
    other_down = jnp.concatenate([down_top[0], down_low[0]], axis=0)

    def half(rows, gate, up):
        gate_acts = jnp.dot(rows, gate[0], preferred_element_type=F32)
        up_acts = jnp.dot(rows, up[0], preferred_element_type=F32)
        return (gate_acts / (1.0 + jnp.exp(-gate_acts)) * up_acts).astype(BF)

    def block(number, carry):
        at = pl.ds(pl.multiple_of(number * BLOCK, BLOCK), BLOCK)
        rows = rows_ref[at]
        own = half(rows, gate_ref, up_ref)
        other = half(rows, other_gate, other_up)
        one = jnp.dot(own, down_ref[0], preferred_element_type=F32).astype(BF)
        two = jnp.dot(other, other_down, preferred_element_type=F32).astype(BF)
        out_ref[at] = (one.astype(F32) + two.astype(F32)).astype(BF)
        return carry

    lax.fori_loop(0, rows_ref.shape[0] // BLOCK, block, 0)


def experts_apply(rows, gate, up, down, swapped):
    vmem = pl.BlockSpec(memory_space=pltpu.VMEM)
    return pl.pallas_call(
        expert_kernel,
        out_shape=jax.ShapeDtypeStruct(rows.shape, BF),
        in_specs=[vmem] * 8,
        out_specs=vmem,
        compiler_params=pltpu.CompilerParams(vmem_limit_bytes=32 << 20),
        cost_estimate=pl.CostEstimate(
            flops=12 * rows.shape[0] * D * gate.shape[2],
            bytes_accessed=12 * D * gate.shape[2] + 4 * rows.shape[0] * D,
            transcendentals=2 * rows.shape[0] * gate.shape[2],
        ),
    )(rows, gate, up, down, *swapped)


def shards(
    residual,
    query_states,
    key_states,
    value_states,
    out_proj,
    norm_gain,
    w_gate,
    w_up,
    w_down,
    expert_ids,
    route_weights,
):
    n_ctx = lax.axis_size("ctx")
    n_ep = lax.axis_size("ep")
    planes = n_ctx // CORES
    tok = residual.shape[0]
    local_experts = EXPERTS // n_ctx
    ctx_index = lax.axis_index("ctx")
    ep_index = lax.axis_index("ep")
    plane, core = ctx_index // CORES, ctx_index % CORES
    kv_head = ep_index * KVH // n_ep
    far = planes // 2
    side = 4
    turn_x, turn_y = ep_index // side, ep_index % side

    def z_perm(step):
        return [
            (z * CORES + c, ((z + step) % planes) * CORES + c)
            for z in range(planes)
            for c in range(CORES)
        ]

    up_perm, down_perm = z_perm(1), z_perm(-1)
    core_perm = [(i, i ^ 1) for i in range(n_ctx)]
    pair_perm = [(i, i ^ 1) for i in range(n_ep)]
    y_perms = [
        [(x * side + y, x * side + (y + step) % side) for x in range(side) for y in range(side)]
        for step in (1, -1)
    ]
    x_perms = [
        [(x * side + y, (x + step) % side * side + y) for x in range(side) for y in range(side)]
        for step in (1, -1)
    ]

    def up(x):
        return lax.ppermute(x, "ctx", up_perm)

    def down(x):
        return lax.ppermute(x, "ctx", down_perm)

    def across(x):
        return lax.ppermute(x, "ctx", core_perm)

    def swap(x):
        return lax.ppermute(x, "ep", pair_perm)

    tie = lax.optimization_barrier

    offsets = [0]
    for step in range(1, far):
        offsets += [-step, step]
    offsets.append(far)

    def shard_id(offset, other):
        return ((plane + offset) % planes) * CORES + jnp.bitwise_xor(core, other)

    key_rows = key_states.shape[0]
    kv_own = stage(
        kv_head.astype(jnp.int32).reshape(1),
        key_states,
        value_states,
        expert_ids.T,
        route_weights.T,
    )

    def ids_of(other, offs):
        ids = [jnp.bitwise_xor(ctx_index, other)] + [shard_id(o, 0) for o in offs]
        return jnp.stack(ids).astype(jnp.int32)

    query_other = across(query_states)
    queries = (query_states, query_other)
    tables = [kv_own]
    states = [None, None]
    above, below = up(kv_own), down(kv_own)
    gate_other = swap(w_gate)
    two_y = [(x * side + y, x * side + (y + 2) % side) for x in range(side) for y in range(side)]
    two_x = [(x * side + y, (x + 2) % side * side + y) for x in range(side) for y in range(side)]
    proj = [lax.ppermute(out_proj, "ep", perm) for perm in x_perms]
    states[0] = attend(ids_of(0, []), queries[0], [kv_own], None, diagonal=True)
    states[1] = attend(ids_of(1, [0]), queries[1], [kv_own], None)
    for step in range(1, far):
        if step == far - 1:
            above, below, states, gate_other, proj_far = tie(
                (above, below, states, gate_other, proj_far)
            )
            up_other = swap(tie((w_up, above))[0])
        elif step == 2:
            above, below, states, proj = tie((above, below, states, proj))
            cut = HD // 2
            proj_far = [
                lax.ppermute(proj[0][:cut], "ep", x_perms[0]),
                lax.ppermute(proj[1][cut:], "ep", x_perms[1]),
            ]
        else:
            above, below, states = tie((above, below, states))
        held = [above, below]
        tables += held
        if step < far - 1:
            above, below = up(above), down(below)
        else:
            last_top, last_low = up(above[:key_rows]), down(below[key_rows:])
        states[0] = attend(ids_of(0, [-step, step]), queries[0], held, states[0])
        states[1] = attend(ids_of(1, [-step, step]), queries[1], held, states[1])
    last_top, last_low, states = tie((last_top, last_low, states))
    proj = [out_proj, *proj, *proj_far]
    held = [last_top, last_low]
    tables.append(last_low)
    part_other = attend(ids_of(1, [far]), queries[1], held, states[1], split=True, last=True)
    part_joined = across(part_other)
    part_own = attend(ids_of(0, [far]), queries[0], held, states[0], split=True, last=True)
    attended = merge(part_own, part_joined).reshape(side, side * tok, HD)

    def x_chunk(step):
        return lax.dynamic_index_in_dim(attended, (turn_x + step) % side, 0, keepdims=False)

    heads = [
        x_chunk(0),
        lax.ppermute(x_chunk(1), "ep", x_perms[0]),
        lax.ppermute(x_chunk(-1), "ep", x_perms[1]),
        lax.ppermute(x_chunk(2), "ep", two_x),
    ]
    partial = project(heads, proj).reshape(side, tok, D)
    partial, up_other = tie((partial, up_other))
    half = w_down.shape[1] // 2
    down_top = swap(tie((w_down[:, :half], up_other))[0])

    def y_chunk(step):
        return lax.dynamic_index_in_dim(partial, (turn_y + step) % side, 0, keepdims=False)

    projected = y_chunk(0).astype(F32)
    for step, perm in ((2, two_y), (1, y_perms[0]), (-1, y_perms[1])):
        projected = projected + lax.ppermute(y_chunk(step), "ep", perm).astype(F32)
    stream = residual.astype(F32) + projected
    normed = (
        stream * lax.rsqrt(jnp.mean(stream * stream, axis=1, keepdims=True) + 1e-06) * norm_gain
    ).astype(BF)

    select, spread = route(
        ctx_index.astype(jnp.int32).reshape(1), tables, tok, local_experts
    )
    column = planes * CAP
    slots = local_experts * column

    blocks = [normed]
    above = below = normed
    for step in range(1, far):
        above, below = up(above), down(below)
        if step == 2:
            above, below, down_top = tie((above, below, down_top))
            down_low = swap(tie((w_down[:, half:], down_top))[0])
        blocks += [above, below]
    rows = tok // 2
    last_top, last_low = up(above[:rows]), down(below[rows:])
    last_top, last_low, down_low = tie((last_top, last_low, down_low))
    blocks += [last_top, last_low]
    gathered = jnp.concatenate(blocks, axis=0)

    def pack(which):
        return (
            jnp.dot(select[which], gathered, preferred_element_type=F32)
            .astype(BF)
            .reshape(local_experts, column, D)
        )

    def exchange(rows):
        return lax.all_to_all(
            rows.reshape(n_ep, slots // n_ep, D), "ep", split_axis=0, concat_axis=0, tiled=True
        ).reshape(slots, D)

    swapped = (gate_other, up_other, down_top, down_low)
    arrived_other = exchange(across(pack(1)))
    arrived = exchange(tie((pack(0), arrived_other))[0])
    out_other = experts_apply(arrived_other, w_gate, w_up, w_down, swapped)
    returned_other = exchange(tie((out_other, arrived))[0])
    out = experts_apply(arrived, w_gate, w_up, w_down, swapped)
    returned = exchange(tie((out, returned_other))[0])
    returned_other = across(returned_other)

    def contract(table, rows):
        return lax.dot_general(table, rows, (((0,), (0,)), ((), ())), preferred_element_type=F32)

    sums = contract(spread[0], returned) + contract(spread[1], returned_other)
    sums = sums.reshape(planes, tok, D)
    at = {offset: number for number, offset in enumerate(offsets)}
    cut = D // 2
    going_down = down(sums[at[far], :, :cut].astype(BF))
    going_up = up(sums[at[far], :, cut:].astype(BF))
    for step in range(far - 1, 0, -1):
        low, high = sums[at[-step]], sums[at[step]]
        if step == far - 1:
            low = jnp.concatenate([low[:, :cut] + going_down.astype(F32), low[:, cut:]], axis=1)
            high = jnp.concatenate([high[:, :cut], high[:, cut:] + going_up.astype(F32)], axis=1)
        else:
            low = low + going_down.astype(F32)
            high = high + going_up.astype(F32)
        going_down, going_up = down(low.astype(BF)), up(high.astype(BF))
    mixture = sums[at[0]] + going_down.astype(F32) + going_up.astype(F32)
    return (stream + mixture).astype(BF)


def solution(mesh):
    return jax.shard_map(
        shards,
        mesh=mesh,
        in_specs=(
            P(("ctx", "ep"), None),
            P("ctx", "ep"),
            P("ctx", None),
            P("ctx", None),
            P("ep", None),
            P(),
            P(("ctx", "ep"), None, None),
            P(("ctx", "ep"), None, None),
            P(("ctx", "ep"), None, None),
            P(("ctx", "ep"), None),
            P(("ctx", "ep"), None),
        ),
        out_specs=P(("ctx", "ep"), None),
        check_vma=False,
    )
```

```python
import functools
import math

import jax
import jax.numpy as jnp
from jax import lax
from jax.experimental import pallas as pl
from jax.experimental.pallas import tpu as pltpu
from jax.sharding import PartitionSpec as P

D = 2048
HD = 128
KVH = 4
HQ = 16
EXPERTS = 128
TOP = 8
CAP = 6
ROWS = 512
CORES = 2
BF = jnp.bfloat16
F32 = jnp.float32
TABLE = 32
NO_COST = pl.CostEstimate(flops=0, bytes_accessed=0, transcendentals=0)
LOG2_SCALE = math.log2(math.e) / math.sqrt(HD)


def attention_step(shards_in, split, diagonal, fresh, last, *refs):
    ids_ref, q_ref = refs[0], refs[1]
    if split:
        kv_refs = [(refs[2], refs[3], 0)]
        rest = refs[4:]
    else:
        kv_refs = [(ref, ref, 2 * ROWS) for ref in refs[2 : 2 + shards_in]]
        rest = refs[2 + shards_in :]
    if not fresh:
        m_in, l_in, a_in = rest[:3]
        rest = rest[3:]
    if last:
        out_ref, m_ref, l_ref, a_ref = rest
    else:
        m_ref, l_ref, a_ref = rest
    own = ids_ref[0]
    if not fresh:
        m_ref[...] = m_in[...]
        l_ref[...] = l_in[...]
        a_ref[...] = a_in[...]
    elif not diagonal:
        m_ref[...] = jnp.full(m_ref.shape, -1e30, F32)
        l_ref[...] = jnp.zeros(l_ref.shape, F32)
        a_ref[...] = jnp.zeros(a_ref.shape, F32)

    def start_of(half):
        return half * ROWS if isinstance(half, int) else pl.multiple_of(half * ROWS, ROWS)

    def tile(slot, half, kv, part, new, masked):
        key_ref, value_ref, values_at = kv
        query = q_ref[pl.ds(start_of(half), ROWS)]
        offset = start_of(part)
        key = key_ref[pl.ds(offset, ROWS)]
        value = value_ref[pl.ds(values_at + offset, ROWS)]
        scores = (
            lax.dot_general(key, query, (((1,), (1,)), ((), ())), preferred_element_type=F32)
            * LOG2_SCALE
        )
        if masked:
            key_at = lax.broadcasted_iota(jnp.int32, scores.shape, 0)
            query_at = lax.broadcasted_iota(jnp.int32, scores.shape, 1)
            scores = jnp.where(key_at <= query_at, scores, -1e30)
        top = jnp.max(scores, axis=0, keepdims=True)
        if not new:
            old = m_ref[slot]
            top = jnp.maximum(old, top)
            correction = jnp.exp2(old - top)
        weights = jnp.exp2(scores - top)
        total = jnp.sum(weights, axis=0, keepdims=True)
        mixed = lax.dot_general(
            value, weights.astype(BF), (((0,), (0,)), ((), ())), preferred_element_type=F32
        )
        if not new:
            total = l_ref[slot] * correction + total
            mixed = a_ref[slot] * correction + mixed
        m_ref[slot] = top
        l_ref[slot] = total
        a_ref[slot] = mixed

    for at in range(shards_in):
        if diagonal:
            tile(0, 0, kv_refs[0], 0, True, True)
            tile(1, 1, kv_refs[0], 1, True, True)
            tile(2, 1, kv_refs[0], 0, True, False)
            continue
        early = ids_ref[1 + at] < own
        half = jnp.where(early, 0, 1)
        tile(2, 1, kv_refs[at], 0, False, False)
        tile(half, half, kv_refs[at], jnp.where(early, 0, 1), False, False)
    if last:
        top = jnp.maximum(m_ref[1], m_ref[2])
        one = jnp.exp2(m_ref[1] - top)
        two = jnp.exp2(m_ref[2] - top)
        out_ref[0, 0:HD] = a_ref[0]
        out_ref[0, HD : HD + 8] = jnp.broadcast_to(m_ref[0], (8, ROWS))
        out_ref[0, HD + 8 : HD + 16] = jnp.broadcast_to(l_ref[0], (8, ROWS))
        out_ref[1, 0:HD] = a_ref[1] * one + a_ref[2] * two
        out_ref[1, HD : HD + 8] = jnp.broadcast_to(top, (8, ROWS))
        out_ref[1, HD + 8 : HD + 16] = jnp.broadcast_to(
            l_ref[1] * one + l_ref[2] * two, (8, ROWS)
        )


def attend(ids, query, shards_kv, state, diagonal=False, split=False, last=False):
    fresh = state is None
    count = 1 if split else len(shards_kv)
    vmem = pl.BlockSpec(memory_space=pltpu.VMEM)
    state_shapes = ((3, 1, ROWS), (3, 1, ROWS), (3, HD, ROWS))
    operands = [ids, query, *shards_kv] + ([] if fresh else list(state))
    if last:
        out_shape = jax.ShapeDtypeStruct((2, HD + 16, ROWS), F32)
        out_specs = vmem
        scratch = [pltpu.VMEM(shape, F32) for shape in state_shapes]
    else:
        out_shape = [jax.ShapeDtypeStruct(shape, F32) for shape in state_shapes]
        out_specs = [vmem] * 3
        scratch = []
    return pl.pallas_call(
        functools.partial(attention_step, count, split, diagonal, fresh, last),
        out_shape=out_shape,
        in_specs=[pl.BlockSpec(memory_space=pltpu.SMEM)] + [vmem] * (len(operands) - 1),
        out_specs=out_specs,
        scratch_shapes=scratch,
        compiler_params=pltpu.CompilerParams(vmem_limit_bytes=16 << 20),
        cost_estimate=pl.CostEstimate(
            flops=24 * count * ROWS * ROWS * HD, bytes_accessed=0, transcendentals=0
        ),
    )(*operands)


def merge_kernel(one_ref, two_ref, out_ref):
    for half in range(2):
        top_one, top_two = one_ref[half, HD : HD + 1], two_ref[half, HD : HD + 1]
        top = jnp.maximum(top_one, top_two)
        one, two = jnp.exp2(top_one - top), jnp.exp2(top_two - top)
        total = one_ref[half, HD + 8 : HD + 9] * one + two_ref[half, HD + 8 : HD + 9] * two
        mixed = one_ref[half, 0:HD] * one + two_ref[half, 0:HD] * two
        rows = (mixed / total).T.astype(BF)
        out_ref[half * ROWS : (half + 1) * ROWS] = rows


def merge(one, two):
    vmem = pl.BlockSpec(memory_space=pltpu.VMEM)
    return pl.pallas_call(
        merge_kernel,
        out_shape=jax.ShapeDtypeStruct((2 * ROWS, HD), BF),
        in_specs=[vmem, vmem],
        out_specs=vmem,
        compiler_params=pltpu.CompilerParams(vmem_limit_bytes=16 << 20),
        cost_estimate=NO_COST,
    )(one, two)


def stage_kernel(head_ref, key_ref, value_ref, ids_ref, gain_ref, out_ref):
    rows = key_ref.shape[0]
    out_ref[0:rows] = key_ref[...]
    out_ref[rows : 2 * rows] = value_ref[...]
    tok = ids_ref.shape[1]
    table = jnp.concatenate([ids_ref[...].astype(F32), gain_ref[...]], axis=0)
    out_ref[2 * rows : 2 * rows + TABLE] = jnp.concatenate(
        [
            jnp.concatenate([table, jnp.zeros((TABLE - 2 * TOP, tok), F32)], axis=0),
            jnp.zeros((TABLE, HD - tok), F32),
        ],
        axis=1,
    ).astype(BF)


def stage(head, keys, values, ids, gains):
    rows, tok = keys.shape[0], ids.shape[1]
    column = pl.BlockSpec((rows, HD), lambda i, head: (0, head[0]))
    small = pl.BlockSpec((TOP, tok), lambda i, head: (0, 0))
    return pl.pallas_call(
        stage_kernel,
        grid_spec=pltpu.PrefetchScalarGridSpec(
            num_scalar_prefetch=1,
            grid=(1,),
            in_specs=[column, column, small, small],
            out_specs=pl.BlockSpec((2 * rows + TABLE, HD), lambda i, head: (0, 0)),
        ),
        out_shape=jax.ShapeDtypeStruct((2 * rows + TABLE, HD), BF),
        compiler_params=pltpu.CompilerParams(vmem_limit_bytes=60 << 20),
        cost_estimate=NO_COST,
    )(head, keys, values, ids, gains)


def route_kernel(tok, local, ctx_ref, *refs):
    tables, (select_ref, spread_ref) = refs[:-2], refs[-2:]
    shards_in = len(tables)
    held = [table[...].astype(F32)[:, :tok] for table in tables]
    table = jnp.concatenate(held, axis=1)
    width = shards_in * tok
    own = ctx_ref[0]
    turn = lax.broadcasted_iota(jnp.int32, (CORES * local, width), 0)
    first = jnp.where(turn < local, own * local, (own + 1 - 2 * (own % 2)) * local - local)
    expert = (first + turn).astype(F32)
    chosen = jnp.zeros((CORES * local, width), F32)
    weight = jnp.zeros((CORES * local, width), F32)
    for k in range(TOP):
        hit = table[k : k + 1] == expert
        chosen = chosen + jnp.where(hit, 1.0, 0.0)
        weight = weight + jnp.where(hit, table[TOP + k : TOP + k + 1], 0.0)
    before = lax.broadcasted_iota(jnp.int32, (width, width), 0)
    after = lax.broadcasted_iota(jnp.int32, (width, width), 1)
    earlier = jnp.logical_and(before // tok == after // tok, before < after)
    rank = jnp.dot(
        chosen.astype(BF), earlier.astype(F32).astype(BF), preferred_element_type=F32
    )
    shard = lax.broadcasted_iota(jnp.int32, (CORES * local, width), 1) // tok
    slot = jnp.where(chosen > 0.5, rank + (shard * CAP).astype(F32), -1.0)
    column = shards_in * CAP
    row = lax.broadcasted_iota(jnp.int32, (column, width), 0).astype(F32)
    for number in range(CORES * local):
        at = slice(number % local * column, (number % local + 1) * column)
        here = row == slot[number : number + 1]
        group = number // local
        select_ref[group, at] = jnp.where(here, 1.0, 0.0).astype(BF)
        spread_ref[group, at] = jnp.where(here, weight[number : number + 1], 0.0).astype(BF)


def route(ctx, tables, tok, local):
    slots, width = local * len(tables) * CAP, len(tables) * tok
    shape = (CORES, slots, width)
    in_specs = [
        pl.BlockSpec(
            (TABLE, HD), functools.partial(lambda last, i, ctx: (last, 0), table.shape[0] // TABLE - 1)
        )
        for table in tables
    ]
    return pl.pallas_call(
        functools.partial(route_kernel, tok, local),
        grid_spec=pltpu.PrefetchScalarGridSpec(
            num_scalar_prefetch=1,
            grid=(1,),
            in_specs=in_specs,
            out_specs=[pl.BlockSpec(shape, lambda i, ctx: (0, 0, 0))] * 2,
        ),
        out_shape=[jax.ShapeDtypeStruct(shape, BF)] * 2,
        compiler_params=pltpu.CompilerParams(vmem_limit_bytes=32 << 20),
        cost_estimate=NO_COST,
    )(ctx, *tables)


def project_kernel(*refs):
    heads, proj, out_ref = refs[:4], refs[4:9], refs[9]
    tables = [proj[0][...], proj[1][...], proj[2][...]]
    tables.append(jnp.concatenate([proj[3][...], proj[4][...]], axis=0))
    total = None
    for pair in ((0, 1), (2, 3)):
        rows = jnp.concatenate([heads[at][...] for at in pair], axis=1)
        table = jnp.concatenate([tables[at] for at in pair], axis=0)
        part = jnp.dot(rows, table, preferred_element_type=F32)
        total = part if total is None else total + part
    out_ref[...] = total.astype(BF)


def project(heads, proj):
    vmem = pl.BlockSpec(memory_space=pltpu.VMEM)
    return pl.pallas_call(
        project_kernel,
        out_shape=jax.ShapeDtypeStruct((heads[0].shape[0], D), BF),
        in_specs=[vmem] * 9,
        out_specs=vmem,
        compiler_params=pltpu.CompilerParams(vmem_limit_bytes=60 << 20),
        cost_estimate=NO_COST,
    )(*heads, *proj)


BLOCK = 384


def expert_kernel(rows_ref, gate_ref, up_ref, down_ref, *refs):
    other_gate, other_up, down_top, down_low, out_ref = refs
    other_down = jnp.concatenate([down_top[0], down_low[0]], axis=0)

    def half(rows, gate, up):
        gate_acts = jnp.dot(rows, gate[0], preferred_element_type=F32)
        up_acts = jnp.dot(rows, up[0], preferred_element_type=F32)
        return (gate_acts / (1.0 + jnp.exp(-gate_acts)) * up_acts).astype(BF)

    def block(number, carry):
        at = pl.ds(pl.multiple_of(number * BLOCK, BLOCK), BLOCK)
        rows = rows_ref[at]
        own = half(rows, gate_ref, up_ref)
        other = half(rows, other_gate, other_up)
        one = jnp.dot(own, down_ref[0], preferred_element_type=F32).astype(BF)
        two = jnp.dot(other, other_down, preferred_element_type=F32).astype(BF)
        out_ref[at] = (one.astype(F32) + two.astype(F32)).astype(BF)
        return carry

    lax.fori_loop(0, rows_ref.shape[0] // BLOCK, block, 0)


def experts_apply(rows, gate, up, down, swapped):
    vmem = pl.BlockSpec(memory_space=pltpu.VMEM)
    return pl.pallas_call(
        expert_kernel,
        out_shape=jax.ShapeDtypeStruct(rows.shape, BF),
        in_specs=[vmem] * 8,
        out_specs=vmem,
        compiler_params=pltpu.CompilerParams(vmem_limit_bytes=32 << 20),
        cost_estimate=pl.CostEstimate(
            flops=12 * rows.shape[0] * D * gate.shape[2],
            bytes_accessed=12 * D * gate.shape[2] + 4 * rows.shape[0] * D,
            transcendentals=2 * rows.shape[0] * gate.shape[2],
        ),
    )(rows, gate, up, down, *swapped)


def shards(
    residual,
    query_states,
    key_states,
    value_states,
    out_proj,
    norm_gain,
    w_gate,
    w_up,
    w_down,
    expert_ids,
    route_weights,
):
    n_ctx = lax.axis_size("ctx")
    n_ep = lax.axis_size("ep")
    planes = n_ctx // CORES
    tok = residual.shape[0]
    local_experts = EXPERTS // n_ctx
    ctx_index = lax.axis_index("ctx")
    ep_index = lax.axis_index("ep")
    plane, core = ctx_index // CORES, ctx_index % CORES
    kv_head = ep_index * KVH // n_ep
    far = planes // 2
    side = 4
    turn_x, turn_y = ep_index // side, ep_index % side

    def z_perm(step):
        return [
            (z * CORES + c, ((z + step) % planes) * CORES + c)
            for z in range(planes)
            for c in range(CORES)
        ]

    up_perm, down_perm = z_perm(1), z_perm(-1)
    core_perm = [(i, i ^ 1) for i in range(n_ctx)]
    pair_perm = [(i, i ^ 1) for i in range(n_ep)]
    y_perms = [
        [(x * side + y, x * side + (y + step) % side) for x in range(side) for y in range(side)]
        for step in (1, -1)
    ]
    x_perms = [
        [(x * side + y, (x + step) % side * side + y) for x in range(side) for y in range(side)]
        for step in (1, -1)
    ]

    def up(x):
        return lax.ppermute(x, "ctx", up_perm)

    def down(x):
        return lax.ppermute(x, "ctx", down_perm)

    def across(x):
        return lax.ppermute(x, "ctx", core_perm)

    def swap(x):
        return lax.ppermute(x, "ep", pair_perm)

    tie = lax.optimization_barrier

    offsets = [0]
    for step in range(1, far):
        offsets += [-step, step]
    offsets.append(far)

    def shard_id(offset, other):
        return ((plane + offset) % planes) * CORES + jnp.bitwise_xor(core, other)

    key_rows = key_states.shape[0]
    kv_own = stage(
        kv_head.astype(jnp.int32).reshape(1),
        key_states,
        value_states,
        expert_ids.T,
        route_weights.T,
    )

    def ids_of(other, offs):
        ids = [jnp.bitwise_xor(ctx_index, other)] + [shard_id(o, 0) for o in offs]
        return jnp.stack(ids).astype(jnp.int32)

    query_other = across(query_states)
    queries = (query_states, query_other)
    tables = [kv_own]
    states = [None, None]
    above, below = up(kv_own), down(kv_own)
    gate_other = swap(w_gate)
    two_y = [(x * side + y, x * side + (y + 2) % side) for x in range(side) for y in range(side)]
    two_x = [(x * side + y, (x + 2) % side * side + y) for x in range(side) for y in range(side)]
    proj = [lax.ppermute(out_proj, "ep", perm) for perm in x_perms]
    states[0] = attend(ids_of(0, []), queries[0], [kv_own], None, diagonal=True)
    states[1] = attend(ids_of(1, [0]), queries[1], [kv_own], None)
    for step in range(1, far):
        if step == far - 1:
            above, below, states, gate_other, proj_far = tie(
                (above, below, states, gate_other, proj_far)
            )
            up_other = swap(tie((w_up, above))[0])
        elif step == 2:
            above, below, states, proj = tie((above, below, states, proj))
            cut = HD // 2
            proj_far = [
                lax.ppermute(proj[0][:cut], "ep", x_perms[0]),
                lax.ppermute(proj[1][cut:], "ep", x_perms[1]),
            ]
        else:
            above, below, states = tie((above, below, states))
        held = [above, below]
        tables += held
        if step < far - 1:
            above, below = up(above), down(below)
        else:
            last_top, last_low = up(above[:key_rows]), down(below[key_rows:])
        states[1] = attend(ids_of(1, [-step, step]), queries[1], held, states[1])
        if step < far - 1:
            states[0] = attend(ids_of(0, [-step, step]), queries[0], held, states[0])
    proj = [out_proj, *proj, *proj_far]
    late = held
    held = [last_top, last_low]
    tables.append(last_low)
    part_other = attend(ids_of(1, [far]), queries[1], held, states[1], split=True, last=True)
    states[0] = attend(ids_of(0, [1 - far, far - 1]), queries[0], late, states[0])
    part_other, states[0] = tie((part_other, states[0]))
    part_joined = across(part_other)
    part_own = attend(ids_of(0, [far]), queries[0], held, states[0], split=True, last=True)
    attended = merge(part_own, part_joined).reshape(side, side * tok, HD)

    def x_chunk(step):
        return lax.dynamic_index_in_dim(attended, (turn_x + step) % side, 0, keepdims=False)

    heads = [
        x_chunk(0),
        lax.ppermute(x_chunk(1), "ep", x_perms[0]),
        lax.ppermute(x_chunk(-1), "ep", x_perms[1]),
        lax.ppermute(x_chunk(2), "ep", two_x),
    ]
    partial = project(heads, proj).reshape(side, tok, D)
    partial, up_other = tie((partial, up_other))
    half = w_down.shape[1] // 2
    down_top = swap(tie((w_down[:, :half], up_other))[0])

    def y_chunk(step):
        return lax.dynamic_index_in_dim(partial, (turn_y + step) % side, 0, keepdims=False)

    projected = y_chunk(0).astype(F32)
    for step, perm in ((2, two_y), (1, y_perms[0]), (-1, y_perms[1])):
        projected = projected + lax.ppermute(y_chunk(step), "ep", perm).astype(F32)
    stream = residual.astype(F32) + projected
    normed = (
        stream * lax.rsqrt(jnp.mean(stream * stream, axis=1, keepdims=True) + 1e-06) * norm_gain
    ).astype(BF)

    select, spread = route(
        ctx_index.astype(jnp.int32).reshape(1), tables, tok, local_experts
    )
    column = planes * CAP
    slots = local_experts * column

    blocks = [normed]
    above = below = normed
    for step in range(1, far):
        above, below = up(above), down(below)
        if step == 2:
            above, below, down_top = tie((above, below, down_top))
            down_low = swap(tie((w_down[:, half:], down_top))[0])
        blocks += [above, below]
    rows = tok // 2
    last_top, last_low = up(above[:rows]), down(below[rows:])
    last_top, last_low, down_low = tie((last_top, last_low, down_low))
    blocks += [last_top, last_low]
    gathered = jnp.concatenate(blocks, axis=0)

    def pack(which, gathered):
        return (
            jnp.dot(select[which], gathered, preferred_element_type=F32)
            .astype(BF)
            .reshape(local_experts, column, D)
        )

    def exchange(rows):
        return lax.all_to_all(
            rows.reshape(n_ep, slots // n_ep, D), "ep", split_axis=0, concat_axis=0, tiled=True
        ).reshape(slots, D)

    swapped = (gate_other, up_other, down_top, down_low)
    packed, gathered = tie((pack(0, gathered), gathered))
    arrived = exchange(packed)
    crossed = across(pack(1, gathered))
    arrived_other = exchange(tie((crossed, arrived))[0])
    out = experts_apply(arrived, w_gate, w_up, w_down, swapped)
    returned = exchange(tie((out, arrived_other))[0])
    out_other = experts_apply(arrived_other, w_gate, w_up, w_down, swapped)
    returned_other = across(exchange(tie((out_other, returned))[0]))

    def contract(table, rows):
        return lax.dot_general(table, rows, (((0,), (0,)), ((), ())), preferred_element_type=F32)

    sums = contract(spread[0], returned) + contract(spread[1], returned_other)
    sums = sums.reshape(planes, tok, D)
    at = {offset: number for number, offset in enumerate(offsets)}
    cut = D // 2
    going_down = down(sums[at[far], :, :cut].astype(BF))
    going_up = up(sums[at[far], :, cut:].astype(BF))
    for step in range(far - 1, 0, -1):
        low, high = sums[at[-step]], sums[at[step]]
        if step == far - 1:
            low = jnp.concatenate([low[:, :cut] + going_down.astype(F32), low[:, cut:]], axis=1)
            high = jnp.concatenate([high[:, :cut], high[:, cut:] + going_up.astype(F32)], axis=1)
        else:
            low = low + going_down.astype(F32)
            high = high + going_up.astype(F32)
        going_down, going_up = down(low.astype(BF)), up(high.astype(BF))
    mixture = sums[at[0]] + going_down.astype(F32) + going_up.astype(F32)
    return (stream + mixture).astype(BF)


def solution(mesh):
    return jax.shard_map(
        shards,
        mesh=mesh,
        in_specs=(
            P(("ctx", "ep"), None),
            P("ctx", "ep"),
            P("ctx", None),
            P("ctx", None),
            P("ep", None),
            P(),
            P(("ctx", "ep"), None, None),
            P(("ctx", "ep"), None, None),
            P(("ctx", "ep"), None, None),
            P(("ctx", "ep"), None),
            P(("ctx", "ep"), None),
        ),
        out_specs=P(("ctx", "ep"), None),
        check_vma=False,
    )
```

```python
import functools
import math

import jax
import jax.numpy as jnp
from jax import lax
from jax.experimental import pallas as pl
from jax.experimental.pallas import tpu as pltpu
from jax.sharding import PartitionSpec as P

D = 2048
HD = 128
KVH = 4
HQ = 16
EXPERTS = 128
TOP = 8
CAP = 6
ROWS = 512
CORES = 2
BF = jnp.bfloat16
F32 = jnp.float32
TABLE = 32
NO_COST = pl.CostEstimate(flops=0, bytes_accessed=0, transcendentals=0)
LOG2_SCALE = math.log2(math.e) / math.sqrt(HD)


def attention_step(shards_in, split, diagonal, fresh, last, *refs):
    ids_ref, q_ref = refs[0], refs[1]
    if split:
        kv_refs = [(refs[2], refs[3], 0)]
        rest = refs[4:]
    else:
        kv_refs = [(ref, ref, 2 * ROWS) for ref in refs[2 : 2 + shards_in]]
        rest = refs[2 + shards_in :]
    if not fresh:
        m_in, l_in, a_in = rest[:3]
        rest = rest[3:]
    if last:
        out_ref, m_ref, l_ref, a_ref = rest
    else:
        m_ref, l_ref, a_ref = rest
    own = ids_ref[0]
    if not fresh:
        m_ref[...] = m_in[...]
        l_ref[...] = l_in[...]
        a_ref[...] = a_in[...]
    elif not diagonal:
        m_ref[...] = jnp.full(m_ref.shape, -1e30, F32)
        l_ref[...] = jnp.zeros(l_ref.shape, F32)
        a_ref[...] = jnp.zeros(a_ref.shape, F32)

    def start_of(half):
        return half * ROWS if isinstance(half, int) else pl.multiple_of(half * ROWS, ROWS)

    def tile(slot, half, kv, part, new, masked):
        key_ref, value_ref, values_at = kv
        query = q_ref[pl.ds(start_of(half), ROWS)]
        offset = start_of(part)
        key = key_ref[pl.ds(offset, ROWS)]
        value = value_ref[pl.ds(values_at + offset, ROWS)]
        scores = (
            lax.dot_general(key, query, (((1,), (1,)), ((), ())), preferred_element_type=F32)
            * LOG2_SCALE
        )
        if masked:
            key_at = lax.broadcasted_iota(jnp.int32, scores.shape, 0)
            query_at = lax.broadcasted_iota(jnp.int32, scores.shape, 1)
            scores = jnp.where(key_at <= query_at, scores, -1e30)
        top = jnp.max(scores, axis=0, keepdims=True)
        if not new:
            old = m_ref[slot]
            top = jnp.maximum(old, top)
            correction = jnp.exp2(old - top)
        weights = jnp.exp2(scores - top)
        total = jnp.sum(weights, axis=0, keepdims=True)
        mixed = lax.dot_general(
            value, weights.astype(BF), (((0,), (0,)), ((), ())), preferred_element_type=F32
        )
        if not new:
            total = l_ref[slot] * correction + total
            mixed = a_ref[slot] * correction + mixed
        m_ref[slot] = top
        l_ref[slot] = total
        a_ref[slot] = mixed

    for at in range(shards_in):
        if diagonal:
            tile(0, 0, kv_refs[0], 0, True, True)
            tile(1, 1, kv_refs[0], 1, True, True)
            tile(2, 1, kv_refs[0], 0, True, False)
            continue
        early = ids_ref[1 + at] < own
        half = jnp.where(early, 0, 1)
        tile(2, 1, kv_refs[at], 0, False, False)
        tile(half, half, kv_refs[at], jnp.where(early, 0, 1), False, False)
    if last:
        top = jnp.maximum(m_ref[1], m_ref[2])
        one = jnp.exp2(m_ref[1] - top)
        two = jnp.exp2(m_ref[2] - top)
        out_ref[0, 0:HD] = a_ref[0]
        out_ref[0, HD : HD + 8] = jnp.broadcast_to(m_ref[0], (8, ROWS))
        out_ref[0, HD + 8 : HD + 16] = jnp.broadcast_to(l_ref[0], (8, ROWS))
        out_ref[1, 0:HD] = a_ref[1] * one + a_ref[2] * two
        out_ref[1, HD : HD + 8] = jnp.broadcast_to(top, (8, ROWS))
        out_ref[1, HD + 8 : HD + 16] = jnp.broadcast_to(
            l_ref[1] * one + l_ref[2] * two, (8, ROWS)
        )


def attend(ids, query, shards_kv, state, diagonal=False, split=False, last=False):
    fresh = state is None
    count = 1 if split else len(shards_kv)
    vmem = pl.BlockSpec(memory_space=pltpu.VMEM)
    state_shapes = ((3, 1, ROWS), (3, 1, ROWS), (3, HD, ROWS))
    operands = [ids, query, *shards_kv] + ([] if fresh else list(state))
    if last:
        out_shape = jax.ShapeDtypeStruct((2, HD + 16, ROWS), F32)
        out_specs = vmem
        scratch = [pltpu.VMEM(shape, F32) for shape in state_shapes]
    else:
        out_shape = [jax.ShapeDtypeStruct(shape, F32) for shape in state_shapes]
        out_specs = [vmem] * 3
        scratch = []
    return pl.pallas_call(
        functools.partial(attention_step, count, split, diagonal, fresh, last),
        out_shape=out_shape,
        in_specs=[pl.BlockSpec(memory_space=pltpu.SMEM)] + [vmem] * (len(operands) - 1),
        out_specs=out_specs,
        scratch_shapes=scratch,
        compiler_params=pltpu.CompilerParams(vmem_limit_bytes=16 << 20),
        cost_estimate=pl.CostEstimate(
            flops=24 * count * ROWS * ROWS * HD, bytes_accessed=0, transcendentals=0
        ),
    )(*operands)


def merge_kernel(one_ref, two_ref, out_ref):
    for half in range(2):
        top_one, top_two = one_ref[half, HD : HD + 1], two_ref[half, HD : HD + 1]
        top = jnp.maximum(top_one, top_two)
        one, two = jnp.exp2(top_one - top), jnp.exp2(top_two - top)
        total = one_ref[half, HD + 8 : HD + 9] * one + two_ref[half, HD + 8 : HD + 9] * two
        mixed = one_ref[half, 0:HD] * one + two_ref[half, 0:HD] * two
        rows = (mixed / total).T.astype(BF)
        out_ref[half * ROWS : (half + 1) * ROWS] = rows


def merge(one, two):
    vmem = pl.BlockSpec(memory_space=pltpu.VMEM)
    return pl.pallas_call(
        merge_kernel,
        out_shape=jax.ShapeDtypeStruct((2 * ROWS, HD), BF),
        in_specs=[vmem, vmem],
        out_specs=vmem,
        compiler_params=pltpu.CompilerParams(vmem_limit_bytes=16 << 20),
        cost_estimate=NO_COST,
    )(one, two)


def stage_kernel(head_ref, key_ref, value_ref, ids_ref, gain_ref, out_ref):
    rows = key_ref.shape[0]
    out_ref[0:rows] = key_ref[...]
    out_ref[rows : 2 * rows] = value_ref[...]
    tok = ids_ref.shape[1]
    table = jnp.concatenate([ids_ref[...].astype(F32), gain_ref[...]], axis=0)
    out_ref[2 * rows : 2 * rows + TABLE] = jnp.concatenate(
        [
            jnp.concatenate([table, jnp.zeros((TABLE - 2 * TOP, tok), F32)], axis=0),
            jnp.zeros((TABLE, HD - tok), F32),
        ],
        axis=1,
    ).astype(BF)


def stage(head, keys, values, ids, gains):
    rows, tok = keys.shape[0], ids.shape[1]
    column = pl.BlockSpec((rows, HD), lambda i, head: (0, head[0]))
    small = pl.BlockSpec((TOP, tok), lambda i, head: (0, 0))
    return pl.pallas_call(
        stage_kernel,
        grid_spec=pltpu.PrefetchScalarGridSpec(
            num_scalar_prefetch=1,
            grid=(1,),
            in_specs=[column, column, small, small],
            out_specs=pl.BlockSpec((2 * rows + TABLE, HD), lambda i, head: (0, 0)),
        ),
        out_shape=jax.ShapeDtypeStruct((2 * rows + TABLE, HD), BF),
        compiler_params=pltpu.CompilerParams(vmem_limit_bytes=60 << 20),
        cost_estimate=NO_COST,
    )(head, keys, values, ids, gains)


def route_kernel(tok, local, ctx_ref, *refs):
    tables, (select_ref, spread_ref) = refs[:-2], refs[-2:]
    shards_in = len(tables)
    held = [table[...].astype(F32)[:, :tok] for table in tables]
    table = jnp.concatenate(held, axis=1)
    width = shards_in * tok
    own = ctx_ref[0]
    turn = lax.broadcasted_iota(jnp.int32, (CORES * local, width), 0)
    first = jnp.where(turn < local, own * local, (own + 1 - 2 * (own % 2)) * local - local)
    expert = (first + turn).astype(F32)
    chosen = jnp.zeros((CORES * local, width), F32)
    weight = jnp.zeros((CORES * local, width), F32)
    for k in range(TOP):
        hit = table[k : k + 1] == expert
        chosen = chosen + jnp.where(hit, 1.0, 0.0)
        weight = weight + jnp.where(hit, table[TOP + k : TOP + k + 1], 0.0)
    before = lax.broadcasted_iota(jnp.int32, (width, width), 0)
    after = lax.broadcasted_iota(jnp.int32, (width, width), 1)
    earlier = jnp.logical_and(before // tok == after // tok, before < after)
    rank = jnp.dot(
        chosen.astype(BF), earlier.astype(F32).astype(BF), preferred_element_type=F32
    )
    shard = lax.broadcasted_iota(jnp.int32, (CORES * local, width), 1) // tok
    slot = jnp.where(chosen > 0.5, rank + (shard * CAP).astype(F32), -1.0)
    column = shards_in * CAP
    row = lax.broadcasted_iota(jnp.int32, (column, width), 0).astype(F32)
    for number in range(CORES * local):
        at = slice(number % local * column, (number % local + 1) * column)
        here = row == slot[number : number + 1]
        group = number // local
        select_ref[group, at] = jnp.where(here, 1.0, 0.0).astype(BF)
        spread_ref[group, at] = jnp.where(here, weight[number : number + 1], 0.0).astype(BF)


def route(ctx, tables, tok, local):
    slots, width = local * len(tables) * CAP, len(tables) * tok
    shape = (CORES, slots, width)
    in_specs = [
        pl.BlockSpec(
            (TABLE, HD), functools.partial(lambda last, i, ctx: (last, 0), table.shape[0] // TABLE - 1)
        )
        for table in tables
    ]
    return pl.pallas_call(
        functools.partial(route_kernel, tok, local),
        grid_spec=pltpu.PrefetchScalarGridSpec(
            num_scalar_prefetch=1,
            grid=(1,),
            in_specs=in_specs,
            out_specs=[pl.BlockSpec(shape, lambda i, ctx: (0, 0, 0))] * 2,
        ),
        out_shape=[jax.ShapeDtypeStruct(shape, BF)] * 2,
        compiler_params=pltpu.CompilerParams(vmem_limit_bytes=32 << 20),
        cost_estimate=NO_COST,
    )(ctx, *tables)


def project_kernel(*refs):
    heads, proj, out_ref = refs[:4], refs[4:11], refs[11]
    tables = [proj[0][...]]
    for at in (1, 3, 5):
        tables.append(jnp.concatenate([proj[at][...], proj[at + 1][...]], axis=0))
    total = None
    for pair in ((0, 1), (2, 3)):
        rows = jnp.concatenate([heads[at][...] for at in pair], axis=1)
        table = jnp.concatenate([tables[at] for at in pair], axis=0)
        part = jnp.dot(rows, table, preferred_element_type=F32)
        total = part if total is None else total + part
    out_ref[...] = total.astype(BF)


def project(heads, proj):
    vmem = pl.BlockSpec(memory_space=pltpu.VMEM)
    return pl.pallas_call(
        project_kernel,
        out_shape=jax.ShapeDtypeStruct((heads[0].shape[0], D), BF),
        in_specs=[vmem] * 11,
        out_specs=vmem,
        compiler_params=pltpu.CompilerParams(vmem_limit_bytes=60 << 20),
        cost_estimate=NO_COST,
    )(*heads, *proj)


BLOCK = 384


def expert_kernel(rows_ref, gate_ref, up_ref, down_ref, *refs):
    other_gate, other_up, other_down, out_ref = refs

    def half(rows, gate, up):
        gate_acts = jnp.dot(rows, gate[0], preferred_element_type=F32)
        up_acts = jnp.dot(rows, up[0], preferred_element_type=F32)
        return (gate_acts / (1.0 + jnp.exp(-gate_acts)) * up_acts).astype(BF)

    def block(number, carry):
        at = pl.ds(pl.multiple_of(number * BLOCK, BLOCK), BLOCK)
        rows = rows_ref[at]
        own = half(rows, gate_ref, up_ref)
        other = half(rows, other_gate, other_up)
        one = jnp.dot(own, down_ref[0], preferred_element_type=F32).astype(BF)
        two = jnp.dot(other, other_down[0], preferred_element_type=F32).astype(BF)
        out_ref[at] = (one.astype(F32) + two.astype(F32)).astype(BF)
        return carry

    lax.fori_loop(0, rows_ref.shape[0] // BLOCK, block, 0)


def experts_apply(rows, gate, up, down, swapped):
    vmem = pl.BlockSpec(memory_space=pltpu.VMEM)
    return pl.pallas_call(
        expert_kernel,
        out_shape=jax.ShapeDtypeStruct(rows.shape, BF),
        in_specs=[vmem] * 7,
        out_specs=vmem,
        compiler_params=pltpu.CompilerParams(vmem_limit_bytes=32 << 20),
        cost_estimate=pl.CostEstimate(
            flops=12 * rows.shape[0] * D * gate.shape[2],
            bytes_accessed=12 * D * gate.shape[2] + 4 * rows.shape[0] * D,
            transcendentals=2 * rows.shape[0] * gate.shape[2],
        ),
    )(rows, gate, up, down, *swapped)


def shards(
    residual,
    query_states,
    key_states,
    value_states,
    out_proj,
    norm_gain,
    w_gate,
    w_up,
    w_down,
    expert_ids,
    route_weights,
):
    n_ctx = lax.axis_size("ctx")
    n_ep = lax.axis_size("ep")
    planes = n_ctx // CORES
    tok = residual.shape[0]
    local_experts = EXPERTS // n_ctx
    ctx_index = lax.axis_index("ctx")
    ep_index = lax.axis_index("ep")
    plane, core = ctx_index // CORES, ctx_index % CORES
    kv_head = ep_index * KVH // n_ep
    far = planes // 2
    side = 4
    turn_x, turn_y = ep_index // side, ep_index % side

    def z_perm(step):
        return [
            (z * CORES + c, ((z + step) % planes) * CORES + c)
            for z in range(planes)
            for c in range(CORES)
        ]

    up_perm, down_perm = z_perm(1), z_perm(-1)
    core_perm = [(i, i ^ 1) for i in range(n_ctx)]
    pair_perm = [(i, i ^ 1) for i in range(n_ep)]
    y_perms = [
        [(x * side + y, x * side + (y + step) % side) for x in range(side) for y in range(side)]
        for step in (1, -1)
    ]
    x_perms = [
        [(x * side + y, (x + step) % side * side + y) for x in range(side) for y in range(side)]
        for step in (1, -1)
    ]

    def up(x):
        return lax.ppermute(x, "ctx", up_perm)

    def down(x):
        return lax.ppermute(x, "ctx", down_perm)

    def across(x):
        return lax.ppermute(x, "ctx", core_perm)

    def swap(x):
        return lax.ppermute(x, "ep", pair_perm)

    tie = lax.optimization_barrier

    offsets = [0]
    for step in range(1, far):
        offsets += [-step, step]
    offsets.append(far)

    def shard_id(offset, other):
        return ((plane + offset) % planes) * CORES + jnp.bitwise_xor(core, other)

    key_rows = key_states.shape[0]
    kv_own = stage(
        kv_head.astype(jnp.int32).reshape(1),
        key_states,
        value_states,
        expert_ids.T,
        route_weights.T,
    )

    def ids_of(other, offs):
        ids = [jnp.bitwise_xor(ctx_index, other)] + [shard_id(o, 0) for o in offs]
        return jnp.stack(ids).astype(jnp.int32)

    query_other = across(query_states)
    queries = (query_states, query_other)
    tables = [kv_own]
    states = [None, None]
    above, below = up(kv_own), down(kv_own)
    gate_other = swap(w_gate)
    two_y = [(x * side + y, x * side + (y + 2) % side) for x in range(side) for y in range(side)]
    two_x = [(x * side + y, (x + 2) % side * side + y) for x in range(side) for y in range(side)]
    cut = HD // 2
    proj_top, proj_low = out_proj[:cut], out_proj[cut:]
    top_behind, low_ahead = (
        lax.ppermute(proj_top, "ep", x_perms[0]),
        lax.ppermute(proj_low, "ep", x_perms[1]),
    )
    low_behind, top_ahead = (
        lax.ppermute(proj_low, "ep", x_perms[0]),
        lax.ppermute(proj_top, "ep", x_perms[1]),
    )
    proj_far = [
        lax.ppermute(top_behind, "ep", x_perms[0]),
        lax.ppermute(low_ahead, "ep", x_perms[1]),
    ]
    states[0] = attend(ids_of(0, []), queries[0], [kv_own], None, diagonal=True)
    states[1] = attend(ids_of(1, [0]), queries[1], [kv_own], None)
    for step in range(1, far):
        if step == far - 1:
            above, below, states, gate_other, proj_far = tie(
                (above, below, states, gate_other, proj_far)
            )
            up_other = swap(tie((w_up, above))[0])
        else:
            above, below, states = tie((above, below, states))
        held = [above, below]
        tables += held
        if step < far - 1:
            above, below = up(above), down(below)
        else:
            last_top, last_low = up(above[:key_rows]), down(below[key_rows:])
        states[1] = attend(ids_of(1, [-step, step]), queries[1], held, states[1])
        if step < far - 1:
            states[0] = attend(ids_of(0, [-step, step]), queries[0], held, states[0])
    proj = [out_proj, top_behind, low_behind, top_ahead, low_ahead, *proj_far]
    late = held
    held = [last_top, last_low]
    tables.append(last_low)
    part_other = attend(ids_of(1, [far]), queries[1], held, states[1], split=True, last=True)
    states[0] = attend(ids_of(0, [1 - far, far - 1]), queries[0], late, states[0])
    part_other, states[0] = tie((part_other, states[0]))
    part_joined = across(part_other)
    part_own = attend(ids_of(0, [far]), queries[0], held, states[0], split=True, last=True)
    attended = merge(part_own, part_joined).reshape(side, side * tok, HD)

    def x_chunk(step):
        return lax.dynamic_index_in_dim(attended, (turn_x + step) % side, 0, keepdims=False)

    heads = [
        x_chunk(0),
        lax.ppermute(x_chunk(1), "ep", x_perms[0]),
        lax.ppermute(x_chunk(-1), "ep", x_perms[1]),
        lax.ppermute(x_chunk(2), "ep", two_x),
    ]
    partial = project(heads, proj).reshape(side, tok, D)
    partial, up_other = tie((partial, up_other))
    down_other = swap(tie((w_down, up_other))[0])

    def y_chunk(step):
        return lax.dynamic_index_in_dim(partial, (turn_y + step) % side, 0, keepdims=False)

    projected = y_chunk(0).astype(F32)
    for step, perm in ((2, two_y), (1, y_perms[0]), (-1, y_perms[1])):
        projected = projected + lax.ppermute(y_chunk(step), "ep", perm).astype(F32)
    stream = residual.astype(F32) + projected
    normed = (
        stream * lax.rsqrt(jnp.mean(stream * stream, axis=1, keepdims=True) + 1e-06) * norm_gain
    ).astype(BF)

    select, spread = route(
        ctx_index.astype(jnp.int32).reshape(1), tables, tok, local_experts
    )
    column = planes * CAP
    slots = local_experts * column

    blocks = [normed]
    above = below = normed
    for step in range(1, far):
        above, below = up(above), down(below)
        blocks += [above, below]
    rows = tok // 2
    last_top, last_low = up(above[:rows]), down(below[rows:])
    blocks += [last_top, last_low]
    gathered = jnp.concatenate(blocks, axis=0)

    def pack(which, gathered):
        return (
            jnp.dot(select[which], gathered, preferred_element_type=F32)
            .astype(BF)
            .reshape(local_experts, column, D)
        )

    def exchange(rows):
        return lax.all_to_all(
            rows.reshape(n_ep, slots // n_ep, D), "ep", split_axis=0, concat_axis=0, tiled=True
        ).reshape(slots, D)

    packed, gathered = tie((pack(0, gathered), gathered))
    arrived = exchange(packed)
    crossed = across(pack(1, gathered))
    crossed, arrived, down_other = tie((crossed, arrived, down_other))
    swapped = (gate_other, up_other, down_other)
    arrived_other = exchange(crossed)
    out = experts_apply(arrived, w_gate, w_up, w_down, swapped)
    returned = exchange(tie((out, arrived_other))[0])
    out_other = experts_apply(arrived_other, w_gate, w_up, w_down, swapped)
    returned_other = across(exchange(tie((out_other, returned))[0]))

    def contract(table, rows):
        return lax.dot_general(table, rows, (((0,), (0,)), ((), ())), preferred_element_type=F32)

    sums = contract(spread[0], returned) + contract(spread[1], returned_other)
    sums = sums.reshape(planes, tok, D)
    at = {offset: number for number, offset in enumerate(offsets)}
    cut = D // 2
    going_down = down(sums[at[far], :, :cut].astype(BF))
    going_up = up(sums[at[far], :, cut:].astype(BF))
    for step in range(far - 1, 0, -1):
        low, high = sums[at[-step]], sums[at[step]]
        if step == far - 1:
            low = jnp.concatenate([low[:, :cut] + going_down.astype(F32), low[:, cut:]], axis=1)
            high = jnp.concatenate([high[:, :cut], high[:, cut:] + going_up.astype(F32)], axis=1)
        else:
            low = low + going_down.astype(F32)
            high = high + going_up.astype(F32)
        going_down, going_up = down(low.astype(BF)), up(high.astype(BF))
    mixture = sums[at[0]] + going_down.astype(F32) + going_up.astype(F32)
    return (stream + mixture).astype(BF)


def solution(mesh):
    return jax.shard_map(
        shards,
        mesh=mesh,
        in_specs=(
            P(("ctx", "ep"), None),
            P("ctx", "ep"),
            P("ctx", None),
            P("ctx", None),
            P("ep", None),
            P(),
            P(("ctx", "ep"), None, None),
            P(("ctx", "ep"), None, None),
            P(("ctx", "ep"), None, None),
            P(("ctx", "ep"), None),
            P(("ctx", "ep"), None),
        ),
        out_specs=P(("ctx", "ep"), None),
        check_vma=False,
    )
```

```python
import functools
import math

import jax
import jax.numpy as jnp
from jax import lax
from jax.experimental import pallas as pl
from jax.experimental.pallas import tpu as pltpu
from jax.sharding import PartitionSpec as P

D = 2048
HD = 128
KVH = 4
HQ = 16
EXPERTS = 128
TOP = 8
CAP = 6
ROWS = 512
CORES = 2
BF = jnp.bfloat16
F32 = jnp.float32
TABLE = 32
NO_COST = pl.CostEstimate(flops=0, bytes_accessed=0, transcendentals=0)
LOG2_SCALE = math.log2(math.e) / math.sqrt(HD)


def attention_step(shards_in, split, diagonal, fresh, last, *refs):
    ids_ref, q_ref = refs[0], refs[1]
    if split:
        kv_refs = [(refs[2], refs[3], 0)]
        rest = refs[4:]
    else:
        kv_refs = [(ref, ref, 2 * ROWS) for ref in refs[2 : 2 + shards_in]]
        rest = refs[2 + shards_in :]
    if not fresh:
        m_in, l_in, a_in = rest[:3]
        rest = rest[3:]
    if last:
        out_ref, m_ref, l_ref, a_ref = rest
    else:
        m_ref, l_ref, a_ref = rest
    own = ids_ref[0]
    if not fresh:
        m_ref[...] = m_in[...]
        l_ref[...] = l_in[...]
        a_ref[...] = a_in[...]
    elif not diagonal:
        m_ref[...] = jnp.full(m_ref.shape, -1e30, F32)
        l_ref[...] = jnp.zeros(l_ref.shape, F32)
        a_ref[...] = jnp.zeros(a_ref.shape, F32)

    def start_of(half):
        return half * ROWS if isinstance(half, int) else pl.multiple_of(half * ROWS, ROWS)

    def tile(slot, half, kv, part, new, masked):
        key_ref, value_ref, values_at = kv
        query = q_ref[pl.ds(start_of(half), ROWS)]
        offset = start_of(part)
        key = key_ref[pl.ds(offset, ROWS)]
        value = value_ref[pl.ds(values_at + offset, ROWS)]
        scores = (
            lax.dot_general(key, query, (((1,), (1,)), ((), ())), preferred_element_type=F32)
            * LOG2_SCALE
        )
        if masked:
            key_at = lax.broadcasted_iota(jnp.int32, scores.shape, 0)
            query_at = lax.broadcasted_iota(jnp.int32, scores.shape, 1)
            scores = jnp.where(key_at <= query_at, scores, -1e30)
        top = jnp.max(scores, axis=0, keepdims=True)
        if not new:
            old = m_ref[slot]
            top = jnp.maximum(old, top)
            correction = jnp.exp2(old - top)
        weights = jnp.exp2(scores - top)
        total = jnp.sum(weights, axis=0, keepdims=True)
        mixed = lax.dot_general(
            value, weights.astype(BF), (((0,), (0,)), ((), ())), preferred_element_type=F32
        )
        if not new:
            total = l_ref[slot] * correction + total
            mixed = a_ref[slot] * correction + mixed
        m_ref[slot] = top
        l_ref[slot] = total
        a_ref[slot] = mixed

    for at in range(shards_in):
        if diagonal:
            tile(0, 0, kv_refs[0], 0, True, True)
            tile(1, 1, kv_refs[0], 1, True, True)
            tile(2, 1, kv_refs[0], 0, True, False)
            continue
        early = ids_ref[1 + at] < own
        half = jnp.where(early, 0, 1)
        tile(2, 1, kv_refs[at], 0, False, False)
        tile(half, half, kv_refs[at], jnp.where(early, 0, 1), False, False)
    if last:
        top = jnp.maximum(m_ref[1], m_ref[2])
        one = jnp.exp2(m_ref[1] - top)
        two = jnp.exp2(m_ref[2] - top)
        out_ref[0, 0:HD] = a_ref[0]
        out_ref[0, HD : HD + 8] = jnp.broadcast_to(m_ref[0], (8, ROWS))
        out_ref[0, HD + 8 : HD + 16] = jnp.broadcast_to(l_ref[0], (8, ROWS))
        out_ref[1, 0:HD] = a_ref[1] * one + a_ref[2] * two
        out_ref[1, HD : HD + 8] = jnp.broadcast_to(top, (8, ROWS))
        out_ref[1, HD + 8 : HD + 16] = jnp.broadcast_to(
            l_ref[1] * one + l_ref[2] * two, (8, ROWS)
        )


def attend(ids, query, shards_kv, state, diagonal=False, split=False, last=False):
    fresh = state is None
    count = 1 if split else len(shards_kv)
    vmem = pl.BlockSpec(memory_space=pltpu.VMEM)
    state_shapes = ((3, 1, ROWS), (3, 1, ROWS), (3, HD, ROWS))
    operands = [ids, query, *shards_kv] + ([] if fresh else list(state))
    if last:
        out_shape = jax.ShapeDtypeStruct((2, HD + 16, ROWS), F32)
        out_specs = vmem
        scratch = [pltpu.VMEM(shape, F32) for shape in state_shapes]
    else:
        out_shape = [jax.ShapeDtypeStruct(shape, F32) for shape in state_shapes]
        out_specs = [vmem] * 3
        scratch = []
    return pl.pallas_call(
        functools.partial(attention_step, count, split, diagonal, fresh, last),
        out_shape=out_shape,
        in_specs=[pl.BlockSpec(memory_space=pltpu.SMEM)] + [vmem] * (len(operands) - 1),
        out_specs=out_specs,
        scratch_shapes=scratch,
        compiler_params=pltpu.CompilerParams(vmem_limit_bytes=16 << 20),
        cost_estimate=pl.CostEstimate(
            flops=24 * count * ROWS * ROWS * HD, bytes_accessed=0, transcendentals=0
        ),
    )(*operands)


def merge_kernel(one_ref, two_ref, out_ref):
    for half in range(2):
        top_one, top_two = one_ref[half, HD : HD + 1], two_ref[half, HD : HD + 1]
        top = jnp.maximum(top_one, top_two)
        one, two = jnp.exp2(top_one - top), jnp.exp2(top_two - top)
        total = one_ref[half, HD + 8 : HD + 9] * one + two_ref[half, HD + 8 : HD + 9] * two
        mixed = one_ref[half, 0:HD] * one + two_ref[half, 0:HD] * two
        rows = (mixed / total).T.astype(BF)
        out_ref[half * ROWS : (half + 1) * ROWS] = rows


def merge(one, two):
    vmem = pl.BlockSpec(memory_space=pltpu.VMEM)
    return pl.pallas_call(
        merge_kernel,
        out_shape=jax.ShapeDtypeStruct((2 * ROWS, HD), BF),
        in_specs=[vmem, vmem],
        out_specs=vmem,
        compiler_params=pltpu.CompilerParams(vmem_limit_bytes=16 << 20),
        cost_estimate=NO_COST,
    )(one, two)


def stage_kernel(head_ref, key_ref, value_ref, ids_ref, gain_ref, out_ref):
    rows = key_ref.shape[0]
    out_ref[0:rows] = key_ref[...]
    out_ref[rows : 2 * rows] = value_ref[...]
    tok = ids_ref.shape[1]
    table = jnp.concatenate([ids_ref[...].astype(F32), gain_ref[...]], axis=0)
    out_ref[2 * rows : 2 * rows + TABLE] = jnp.concatenate(
        [
            jnp.concatenate([table, jnp.zeros((TABLE - 2 * TOP, tok), F32)], axis=0),
            jnp.zeros((TABLE, HD - tok), F32),
        ],
        axis=1,
    ).astype(BF)


def stage(head, keys, values, ids, gains):
    rows, tok = keys.shape[0], ids.shape[1]
    column = pl.BlockSpec((rows, HD), lambda i, head: (0, head[0]))
    small = pl.BlockSpec((TOP, tok), lambda i, head: (0, 0))
    return pl.pallas_call(
        stage_kernel,
        grid_spec=pltpu.PrefetchScalarGridSpec(
            num_scalar_prefetch=1,
            grid=(1,),
            in_specs=[column, column, small, small],
            out_specs=pl.BlockSpec((2 * rows + TABLE, HD), lambda i, head: (0, 0)),
        ),
        out_shape=jax.ShapeDtypeStruct((2 * rows + TABLE, HD), BF),
        compiler_params=pltpu.CompilerParams(vmem_limit_bytes=60 << 20),
        cost_estimate=NO_COST,
    )(head, keys, values, ids, gains)


def route_kernel(tok, local, ctx_ref, *refs):
    tables, (select_ref, spread_ref) = refs[:-2], refs[-2:]
    shards_in = len(tables)
    held = [table[...].astype(F32)[:, :tok] for table in tables]
    table = jnp.concatenate(held, axis=1)
    width = shards_in * tok
    own = ctx_ref[0]
    turn = lax.broadcasted_iota(jnp.int32, (CORES * local, width), 0)
    first = jnp.where(turn < local, own * local, (own + 1 - 2 * (own % 2)) * local - local)
    expert = (first + turn).astype(F32)
    chosen = jnp.zeros((CORES * local, width), F32)
    weight = jnp.zeros((CORES * local, width), F32)
    for k in range(TOP):
        hit = table[k : k + 1] == expert
        chosen = chosen + jnp.where(hit, 1.0, 0.0)
        weight = weight + jnp.where(hit, table[TOP + k : TOP + k + 1], 0.0)
    before = lax.broadcasted_iota(jnp.int32, (width, width), 0)
    after = lax.broadcasted_iota(jnp.int32, (width, width), 1)
    earlier = jnp.logical_and(before // tok == after // tok, before < after)
    rank = jnp.dot(
        chosen.astype(BF), earlier.astype(F32).astype(BF), preferred_element_type=F32
    )
    shard = lax.broadcasted_iota(jnp.int32, (CORES * local, width), 1) // tok
    slot = jnp.where(chosen > 0.5, rank + (shard * CAP).astype(F32), -1.0)
    column = shards_in * CAP
    row = lax.broadcasted_iota(jnp.int32, (column, width), 0).astype(F32)
    for number in range(CORES * local):
        at = slice(number % local * column, (number % local + 1) * column)
        here = row == slot[number : number + 1]
        group = number // local
        select_ref[group, at] = jnp.where(here, 1.0, 0.0).astype(BF)
        spread_ref[group, at] = jnp.where(here, weight[number : number + 1], 0.0).astype(BF)


def route(ctx, tables, tok, local):
    slots, width = local * len(tables) * CAP, len(tables) * tok
    shape = (CORES, slots, width)
    in_specs = [
        pl.BlockSpec(
            (TABLE, HD), functools.partial(lambda last, i, ctx: (last, 0), table.shape[0] // TABLE - 1)
        )
        for table in tables
    ]
    return pl.pallas_call(
        functools.partial(route_kernel, tok, local),
        grid_spec=pltpu.PrefetchScalarGridSpec(
            num_scalar_prefetch=1,
            grid=(1,),
            in_specs=in_specs,
            out_specs=[pl.BlockSpec(shape, lambda i, ctx: (0, 0, 0))] * 2,
        ),
        out_shape=[jax.ShapeDtypeStruct(shape, BF)] * 2,
        compiler_params=pltpu.CompilerParams(vmem_limit_bytes=32 << 20),
        cost_estimate=NO_COST,
    )(ctx, *tables)


def project_kernel(*refs):
    turn_ref, heads, proj, outs, total_ref = refs[0], refs[1:5], refs[5:12], refs[12:16], refs[16]
    tables = [proj[0][...]]
    for at in (1, 3, 5):
        tables.append(jnp.concatenate([proj[at][...], proj[at + 1][...]], axis=0))
    total = None
    for pair in ((0, 1), (2, 3)):
        rows = jnp.concatenate([heads[at][...] for at in pair], axis=1)
        table = jnp.concatenate([tables[at] for at in pair], axis=0)
        part = jnp.dot(rows, table, preferred_element_type=F32)
        total = part if total is None else total + part
    total_ref[...] = total
    side = len(outs)
    tok = total.shape[0] // side
    for step, out_ref in enumerate(outs):
        at = pl.multiple_of((turn_ref[0] + step) % side * tok, tok)
        out_ref[...] = total_ref[pl.ds(at, tok)].astype(BF)


def project(turn, heads, proj):
    side = len(heads)
    tok = heads[0].shape[0] // side
    vmem = pl.BlockSpec(memory_space=pltpu.VMEM)
    return pl.pallas_call(
        project_kernel,
        out_shape=[jax.ShapeDtypeStruct((tok, D), BF)] * side,
        in_specs=[pl.BlockSpec(memory_space=pltpu.SMEM)] + [vmem] * 11,
        out_specs=[vmem] * side,
        scratch_shapes=[pltpu.VMEM((side * tok, D), F32)],
        compiler_params=pltpu.CompilerParams(vmem_limit_bytes=60 << 20),
        cost_estimate=NO_COST,
    )(turn, *heads, *proj)


def norm_kernel(residual_ref, gain_ref, one, two, three, four, stream_ref, normed_ref):
    stream = residual_ref[...].astype(F32) + one[...].astype(F32)
    stream = stream + two[...].astype(F32) + three[...].astype(F32) + four[...].astype(F32)
    scale = lax.rsqrt(jnp.mean(stream * stream, axis=1, keepdims=True) + 1e-06)
    stream_ref[...] = stream
    normed_ref[...] = (stream * scale * gain_ref[...]).astype(BF)


def norm(residual, gain, parts):
    vmem = pl.BlockSpec(memory_space=pltpu.VMEM)
    shape = residual.shape
    return pl.pallas_call(
        norm_kernel,
        out_shape=[jax.ShapeDtypeStruct(shape, F32), jax.ShapeDtypeStruct(shape, BF)],
        in_specs=[vmem] * 6,
        out_specs=[vmem] * 2,
        compiler_params=pltpu.CompilerParams(vmem_limit_bytes=16 << 20),
        cost_estimate=NO_COST,
    )(residual, gain.reshape(1, D), *parts)


BLOCK = 384


def expert_kernel(rows_ref, gate_ref, up_ref, down_ref, *refs):
    other_gate, other_up, other_down, out_ref = refs

    def half(rows, gate, up):
        gate_acts = jnp.dot(rows, gate[0], preferred_element_type=F32)
        up_acts = jnp.dot(rows, up[0], preferred_element_type=F32)
        return (gate_acts / (1.0 + jnp.exp(-gate_acts)) * up_acts).astype(BF)

    def block(number, carry):
        at = pl.ds(pl.multiple_of(number * BLOCK, BLOCK), BLOCK)
        rows = rows_ref[at]
        own = half(rows, gate_ref, up_ref)
        other = half(rows, other_gate, other_up)
        one = jnp.dot(own, down_ref[0], preferred_element_type=F32).astype(BF)
        two = jnp.dot(other, other_down[0], preferred_element_type=F32).astype(BF)
        out_ref[at] = (one.astype(F32) + two.astype(F32)).astype(BF)
        return carry

    lax.fori_loop(0, rows_ref.shape[0] // BLOCK, block, 0)


def experts_apply(rows, gate, up, down, swapped):
    vmem = pl.BlockSpec(memory_space=pltpu.VMEM)
    return pl.pallas_call(
        expert_kernel,
        out_shape=jax.ShapeDtypeStruct(rows.shape, BF),
        in_specs=[vmem] * 7,
        out_specs=vmem,
        compiler_params=pltpu.CompilerParams(vmem_limit_bytes=32 << 20),
        cost_estimate=pl.CostEstimate(
            flops=12 * rows.shape[0] * D * gate.shape[2],
            bytes_accessed=12 * D * gate.shape[2] + 4 * rows.shape[0] * D,
            transcendentals=2 * rows.shape[0] * gate.shape[2],
        ),
    )(rows, gate, up, down, *swapped)


def shards(
    residual,
    query_states,
    key_states,
    value_states,
    out_proj,
    norm_gain,
    w_gate,
    w_up,
    w_down,
    expert_ids,
    route_weights,
):
    n_ctx = lax.axis_size("ctx")
    n_ep = lax.axis_size("ep")
    planes = n_ctx // CORES
    tok = residual.shape[0]
    local_experts = EXPERTS // n_ctx
    ctx_index = lax.axis_index("ctx")
    ep_index = lax.axis_index("ep")
    plane, core = ctx_index // CORES, ctx_index % CORES
    kv_head = ep_index * KVH // n_ep
    far = planes // 2
    side = 4
    turn_x, turn_y = ep_index // side, ep_index % side

    def z_perm(step):
        return [
            (z * CORES + c, ((z + step) % planes) * CORES + c)
            for z in range(planes)
            for c in range(CORES)
        ]

    up_perm, down_perm = z_perm(1), z_perm(-1)
    core_perm = [(i, i ^ 1) for i in range(n_ctx)]
    pair_perm = [(i, i ^ 1) for i in range(n_ep)]
    y_perms = [
        [(x * side + y, x * side + (y + step) % side) for x in range(side) for y in range(side)]
        for step in (1, -1)
    ]
    x_perms = [
        [(x * side + y, (x + step) % side * side + y) for x in range(side) for y in range(side)]
        for step in (1, -1)
    ]

    def up(x):
        return lax.ppermute(x, "ctx", up_perm)

    def down(x):
        return lax.ppermute(x, "ctx", down_perm)

    def across(x):
        return lax.ppermute(x, "ctx", core_perm)

    def swap(x):
        return lax.ppermute(x, "ep", pair_perm)

    tie = lax.optimization_barrier

    offsets = [0]
    for step in range(1, far):
        offsets += [-step, step]
    offsets.append(far)

    def shard_id(offset, other):
        return ((plane + offset) % planes) * CORES + jnp.bitwise_xor(core, other)

    key_rows = key_states.shape[0]
    kv_own = stage(
        kv_head.astype(jnp.int32).reshape(1),
        key_states,
        value_states,
        expert_ids.T,
        route_weights.T,
    )

    def ids_of(other, offs):
        ids = [jnp.bitwise_xor(ctx_index, other)] + [shard_id(o, 0) for o in offs]
        return jnp.stack(ids).astype(jnp.int32)

    query_other = across(query_states)
    queries = (query_states, query_other)
    tables = [kv_own]
    states = [None, None]
    above, below = up(kv_own), down(kv_own)
    gate_other = swap(w_gate)
    two_y = [(x * side + y, x * side + (y + 2) % side) for x in range(side) for y in range(side)]
    two_x = [(x * side + y, (x + 2) % side * side + y) for x in range(side) for y in range(side)]
    cut = HD // 2
    proj_top, proj_low = out_proj[:cut], out_proj[cut:]
    top_behind, low_ahead = (
        lax.ppermute(proj_top, "ep", x_perms[0]),
        lax.ppermute(proj_low, "ep", x_perms[1]),
    )
    low_behind, top_ahead = (
        lax.ppermute(proj_low, "ep", x_perms[0]),
        lax.ppermute(proj_top, "ep", x_perms[1]),
    )
    proj_far = [
        lax.ppermute(top_behind, "ep", x_perms[0]),
        lax.ppermute(low_ahead, "ep", x_perms[1]),
    ]
    states[0] = attend(ids_of(0, []), queries[0], [kv_own], None, diagonal=True)
    states[1] = attend(ids_of(1, [0]), queries[1], [kv_own], None)
    for step in range(1, far):
        if step == far - 1:
            above, below, states, gate_other, proj_far = tie(
                (above, below, states, gate_other, proj_far)
            )
            up_other = swap(tie((w_up, above))[0])
        else:
            above, below, states = tie((above, below, states))
        held = [above, below]
        tables += held
        if step < far - 1:
            above, below = up(above), down(below)
        else:
            last_top, last_low = up(above[:key_rows]), down(below[key_rows:])
        states[1] = attend(ids_of(1, [-step, step]), queries[1], held, states[1])
        if step < far - 1:
            states[0] = attend(ids_of(0, [-step, step]), queries[0], held, states[0])
    proj = [out_proj, top_behind, low_behind, top_ahead, low_ahead, *proj_far]
    late = held
    held = [last_top, last_low]
    tables.append(last_low)
    part_other = attend(ids_of(1, [far]), queries[1], held, states[1], split=True, last=True)
    states[0] = attend(ids_of(0, [1 - far, far - 1]), queries[0], late, states[0])
    part_other, states[0] = tie((part_other, states[0]))
    part_joined = across(part_other)
    part_own = attend(ids_of(0, [far]), queries[0], held, states[0], split=True, last=True)
    attended = merge(part_own, part_joined).reshape(side, side * tok, HD)

    def x_chunk(step):
        return lax.dynamic_index_in_dim(attended, (turn_x + step) % side, 0, keepdims=False)

    heads = [
        x_chunk(0),
        lax.ppermute(x_chunk(1), "ep", x_perms[0]),
        lax.ppermute(x_chunk(-1), "ep", x_perms[1]),
        lax.ppermute(x_chunk(2), "ep", two_x),
    ]
    partial = project(turn_y.astype(jnp.int32).reshape(1), heads, proj)
    partial, up_other = tie((partial, up_other))
    down_other = swap(tie((w_down, up_other))[0])
    sent = [(2, two_y), (1, y_perms[0]), (3, y_perms[1])]
    parts = [partial[0]] + [lax.ppermute(partial[step], "ep", perm) for step, perm in sent]
    stream, normed = norm(residual, norm_gain, parts)

    select, spread = route(
        ctx_index.astype(jnp.int32).reshape(1), tables, tok, local_experts
    )
    column = planes * CAP
    slots = local_experts * column

    blocks = [normed]
    above = below = normed
    for step in range(1, far):
        above, below = up(above), down(below)
        blocks += [above, below]
    rows = tok // 2
    last_top, last_low = up(above[:rows]), down(below[rows:])
    blocks += [last_top, last_low]
    gathered = jnp.concatenate(blocks, axis=0)

    def pack(which, gathered):
        return (
            jnp.dot(select[which], gathered, preferred_element_type=F32)
            .astype(BF)
            .reshape(local_experts, column, D)
        )

    def exchange(rows):
        return lax.all_to_all(
            rows.reshape(n_ep, slots // n_ep, D), "ep", split_axis=0, concat_axis=0, tiled=True
        ).reshape(slots, D)

    packed, gathered = tie((pack(0, gathered), gathered))
    arrived = exchange(packed)
    crossed = across(pack(1, gathered))
    crossed, arrived, down_other = tie((crossed, arrived, down_other))
    swapped = (gate_other, up_other, down_other)
    arrived_other = exchange(crossed)
    out = experts_apply(arrived, w_gate, w_up, w_down, swapped)
    returned = exchange(tie((out, arrived_other))[0])
    out_other = experts_apply(arrived_other, w_gate, w_up, w_down, swapped)
    returned_other = exchange(tie((out_other, returned))[0])

    def contract(table, rows):
        return lax.dot_general(table, rows, (((0,), (0,)), ((), ())), preferred_element_type=F32)

    sums, returned_other = tie((contract(spread[0], returned), returned_other))
    sums = sums + contract(spread[1], across(returned_other))
    sums = sums.reshape(planes, tok, D)
    at = {offset: number for number, offset in enumerate(offsets)}
    cut = D // 2
    going_down = down(sums[at[far], :, :cut].astype(BF))
    going_up = up(sums[at[far], :, cut:].astype(BF))
    for step in range(far - 1, 0, -1):
        low, high = sums[at[-step]], sums[at[step]]
        if step == far - 1:
            low = jnp.concatenate([low[:, :cut] + going_down.astype(F32), low[:, cut:]], axis=1)
            high = jnp.concatenate([high[:, :cut], high[:, cut:] + going_up.astype(F32)], axis=1)
        else:
            low = low + going_down.astype(F32)
            high = high + going_up.astype(F32)
        going_down, going_up = down(low.astype(BF)), up(high.astype(BF))
    mixture = sums[at[0]] + going_down.astype(F32) + going_up.astype(F32)
    return (stream + mixture).astype(BF)


def solution(mesh):
    return jax.shard_map(
        shards,
        mesh=mesh,
        in_specs=(
            P(("ctx", "ep"), None),
            P("ctx", "ep"),
            P("ctx", None),
            P("ctx", None),
            P("ep", None),
            P(),
            P(("ctx", "ep"), None, None),
            P(("ctx", "ep"), None, None),
            P(("ctx", "ep"), None, None),
            P(("ctx", "ep"), None),
            P(("ctx", "ep"), None),
        ),
        out_specs=P(("ctx", "ep"), None),
        check_vma=False,
    )
```
